128 devices in a mesh: row: 16 (over x, z), grp: 8 (over y, core).
Axes of the slice: x: 4, y: 4, z: 4, core: 2. Of those that a mesh axis runs over, the one named last changes fastest.
Arguments:
- sketch: bfloat16 [1024, 256, 256], P(('row', 'grp')), may hold values from -6 to 6
- band_tiles: bfloat16 [1024, 3, 256, 256], P(('row', 'grp')), may hold values from -0.125 to 0.125
- far_tiles: bfloat16 [1024, 8, 256, 256], P(('row', 'grp')), may hold values from -0.125 to 0.125
- far_owner: int32 [1024, 8], P(('row', 'grp')), may hold values from 0 to 15, all different within a row; in each aligned block of 8 rows (0 to 7, 8 to 15, ...) at most 6 rows name the same one
- far_local: int32 [1024, 8], P(('row', 'grp')), may hold values from 0 to 7
- far_count: int32 [1024], P(('row', 'grp')), may hold values from 1 to 8, as said below
Outputs:
- basis: float32 [1024, 256, 256], P(('row', 'grp'))
- factor: float32 [256, 256], replicated
The draws below stay inside these ranges and needn't reach their ends.
Inputs may be any that keep to these rules, and one draw needn't show every extreme that they name: `far_owner`: in the 8 block rows of one device, the entries of one row are distinct, and no value is named by more than 6 entries; some value reaches 6. `far_count`: the first block row of every device has 8 live slots.
All inputs are finite; a program needn't handle non-finite values.
Results may differ from the reference program's by a relative error of at most 0.003.
Values may be sent and summed in bfloat16 or wider, within the bound.
A program may use at most 128 MiB of HBM per device.

```python
import math
import jax
import jax.numpy as jnp
import numpy as np
from jax import lax

B = 256
K = 256
LR = 8
BR_DEV = 8
N_BLK = 1024
ROWS = 262144
CAP = 6
N_ROW = 16
N_GRP = 8


def draw_far_count(key, part):
    key = jax.random.fold_in(key, 7)
    counts = jax.random.randint(key, (N_BLK,), 1, LR + 1)
    first_rows = jnp.arange(N_BLK) % BR_DEV == 0
    return jnp.where(first_rows, LR, counts).astype(jnp.int32)


def place_ends(values, own_key, smallest, high):
    longest = values.shape.index(max(values.shape))
    spots = []
    for shift in (0, 1):
        where = [jax.random.randint(jax.random.fold_in(own_key, axis), (), 0, length) for axis, length in enumerate(values.shape)]
        where[longest] = (where[longest] + shift) % values.shape[longest]
        spots.append(tuple(where))
    return values.at[spots[0]].set(smallest).at[spots[1]].set(high)


def shard_levels(rng, extent, shards, low, largest):
    gain = 1.0
    for axis_at, blocks in shards:
        draws = jax.random.uniform(jax.random.fold_in(jax.random.fold_in(rng, 6), axis_at), (blocks,), jnp.float32, low / len(shards), largest / len(shards))
        gain = gain * jnp.repeat(jnp.exp(draws), extent[axis_at] // blocks).reshape((-1,) + (1,) * (len(extent) - 1 - axis_at))
    return gain


def deal_out(stream_key, own, number, rows, amount, top, bound, skew):
    sequence = jax.random.permutation(stream_key, amount)
    packed, common = shares(amount, rows * top, bound, skew, True), shares(amount, rows * top, bound, skew, False)
    places = jnp.arange(amount)

    def named(tallies, turn):
        used = int((tallies > 0).sum())
        fixed = max(1, used // 4)
        moved = fixed + (places - fixed + turn * (used - fixed)) % max(1, amount - fixed)
        return jnp.zeros((amount,), jnp.int32).at[sequence[jnp.where(places < fixed, places, moved)]].set(jnp.asarray(tallies, jnp.int32))

    tallies = jnp.where(number % 4 == 0, named(packed, number // 4), named(common, number - number // 4 - 1))
    mixed = jax.random.permutation(jax.random.fold_in(own, 3), amount)
    donor, receiver = mixed[0:amount // 2 * 2:2], mixed[1:amount // 2 * 2:2]
    slack = jnp.minimum(tallies[donor] - 1, bound - tallies[receiver]) // 2
    slack = jnp.where((donor == sequence[0]) | (receiver == sequence[0]) | (tallies[receiver] == 0), 0, jnp.maximum(slack, 0))
    moved = jax.random.randint(jax.random.fold_in(own, 4), (amount // 2,), 0, 1 << 20) % (slack + 1)
    tallies = tallies.at[donor].add(-moved).at[receiver].add(moved)
    members = jnp.searchsorted(jnp.cumsum(tallies), jnp.arange(rows * top), side="right").astype(jnp.int32)
    grid = members.reshape(top, rows).T
    grid = grid[jax.random.permutation(jax.random.fold_in(own, 1), rows)]
    turn = jax.random.randint(jax.random.fold_in(own, 2), (rows, 1), 0, top)
    return jnp.take_along_axis(grid, (jnp.arange(top)[None, :] + turn) % top, axis=1)


def shares(count, total, most, skew, full):
    weights = [(1 << 20) // math.isqrt(standing ** skew) + 1 for standing in range(1, count + 1)]
    largest = most if full else min(most, max(-(-total // count), total * weights[0] // sum(weights)))
    least = 1 if total - largest >= count - 1 else 0
    holding, rest = [largest] + [least] * (count - 1), total - largest - least * (count - 1)
    while rest > 0:
        movable = [i for i in range(1, count) if holding[i] < largest] or [i for i in range(1, count) if holding[i] < most]
        pool, budget = sum([weights[i] for i in movable]), rest
        for i in movable:
            extra = min(most - holding[i], max(1, budget * weights[i] // pool), rest)
            holding[i] = holding[i] + extra
            rest = rest - extra
    return np.array(holding)


def centred(rng, dims, spread, limit, cuts=(), held_as=jnp.bfloat16):
    values = spread * jax.random.normal(rng, dims, jnp.float32)
    if cuts:
        values = values * shard_levels(rng, dims, cuts, -0.22, 0.18)
    return jnp.clip(values, -limit, limit).astype(held_as)


def setup_inputs(seed: int = 0) -> dict:
    keys = jax.random.split(jax.random.key(seed), 7)
    sketch = centred(keys[0], (N_BLK, B, K), 1.0, 6.0, ((0, 128),))
    band_tiles = centred(keys[1], (N_BLK, 3, B, B), (B * 7) ** -0.5, 0.125, ((0, 128),))
    far_tiles = centred(keys[2], (N_BLK, LR, B, B), (B * 7) ** -0.5, 0.125, ((0, 128),))
    far_owner_keys = jax.random.split(jax.random.fold_in(keys[3], 1), N_BLK // BR_DEV)
    far_owner_turns = jax.random.permutation(jax.random.fold_in(keys[3], 3), N_BLK // BR_DEV)
    far_owner = jax.vmap(lambda own, number: deal_out(jax.random.fold_in(keys[3], 2), own, number, BR_DEV, N_ROW, LR, CAP, 2))(far_owner_keys, far_owner_turns).reshape((N_BLK, LR))
    far_local = place_ends(jax.random.randint(keys[4], (N_BLK, LR), 0, BR_DEV), jax.random.fold_in(keys[4], 1), 0, BR_DEV - 1).astype(jnp.int32)
    far_count = draw_far_count(jax.random.fold_in(keys[6], 71), 0)
    return dict(sketch=sketch, band_tiles=band_tiles, far_tiles=far_tiles, far_owner=far_owner, far_local=far_local, far_count=far_count)


def apply_matrix(band_tiles, far_tiles, columns, live_mask, panel):
    zero_block = jnp.zeros((1,) + panel.shape[1:], panel.dtype)
    padded = jnp.concatenate([zero_block, panel, zero_block], axis=0)

    def one_row(index_row):
        near = lax.dynamic_slice_in_dim(padded, index_row, 3, 0).astype(jnp.float32)
        result = jnp.einsum('sab,sbk->ak', band_tiles[index_row].astype(jnp.float32), near, precision=lax.Precision.HIGHEST)
        remote = panel[columns[index_row]].astype(jnp.float32) * live_mask[index_row][:, None, None]
        result = result + jnp.einsum('sab,sbk->ak', far_tiles[index_row].astype(jnp.float32), remote, precision=lax.Precision.HIGHEST)
        return result
    return lax.map(one_row, jnp.arange(panel.shape[0], dtype=jnp.int32))

def reference(sketch, band_tiles, far_tiles, far_owner, far_local, far_count):
    block_ids = jnp.arange(N_BLK, dtype=jnp.int32)
    group = block_ids // BR_DEV % N_GRP
    columns = ((far_owner * N_GRP + group[:, None]) * BR_DEV + far_local).astype(jnp.int32)
    live_mask = (jnp.arange(LR, dtype=jnp.int32)[None, :] < far_count[:, None]).astype(jnp.float32)
    first = apply_matrix(band_tiles, far_tiles, columns, live_mask, sketch).astype(jnp.bfloat16)
    second = apply_matrix(band_tiles, far_tiles, columns, live_mask, first)
    flat_rows = second.reshape(ROWS, K)
    gram = jnp.dot(flat_rows.T.astype(jnp.float32), flat_rows.astype(jnp.float32), precision=lax.Precision.HIGHEST, preferred_element_type=jnp.float32)
    lower_factor = jnp.linalg.cholesky(gram)
    solved = jax.scipy.linalg.solve_triangular(lower_factor, flat_rows.T, lower=True)
    scale_rows = math.sqrt(ROWS)
    basis = (solved.T * scale_rows).reshape(N_BLK, B, K)
    factor = lower_factor.T / scale_rows
    return (basis, factor)
```

```python
import functools
import math

import jax
import jax.numpy as jnp
from jax import lax
from jax.experimental import pallas as pl
from jax.experimental.pallas import tpu as pltpu
from jax.sharding import PartitionSpec as P

MESH = pl.DeviceIdType.MESH
SIDE = 4
N_ROW = SIDE * SIDE
N_GRP = 8
BLOCKS = 8
SLOTS = 8
B = 256
N_PANEL = N_ROW * BLOCKS
ZERO, LEFT, RIGHT = N_PANEL, N_PANEL + 1, N_PANEL + 2
PART = B // N_ROW
F32 = jnp.float32
BF16 = jnp.bfloat16


def dot(a, b):
    return jnp.dot(a, b, preferred_element_type=F32)


def range_kernel(
    sketch, band, far, owner, local, count,
    second_out, gram_out,
    panel_a, panel_b, band_v, far_v, acc, gram_v, gram_c, parts, shares,
    load_sem, recv_sem, send_sem, halo_send, halo_recv,
    scatter_send, scatter_recv, share_send, share_recv, spread_send, spread_recv, out_sem,
):
    row, grp = lax.axis_index("row"), lax.axis_index("grp")
    x, z = row // SIDE, row % SIDE
    device = row * N_GRP + grp
    after, before = (device + 1) % (N_ROW * N_GRP), (device + N_ROW * N_GRP - 1) % (N_ROW * N_GRP)
    after_id = (after // N_GRP, after % N_GRP)
    before_id = (before // N_GRP, before % N_GRP)
    own = row * BLOCKS

    load_panel = pltpu.make_async_copy(sketch, panel_a.at[pl.ds(own, BLOCKS)], load_sem.at[0])
    load_band = pltpu.make_async_copy(band, band_v, load_sem.at[1])
    load_far = pltpu.make_async_copy(far, far_v, load_sem.at[2])
    load_panel.start()
    load_band.start()
    load_far.start()

    barrier = pltpu.get_barrier_semaphore()

    def greet(device_id):
        pl.semaphore_signal(barrier, inc=1, device_id=device_id, device_id_type=MESH)

    @pl.loop(1, N_ROW)
    def _(k):
        greet(((row + k) % N_ROW, grp))

    @pl.loop(1, N_GRP)
    def _(k):
        greet((row, (grp + k) % N_GRP))

    greet(after_id)
    greet(before_id)
    for panel in (panel_a, panel_b):
        panel[ZERO] = jnp.zeros((B, B), BF16)
    load_panel.wait()
    pl.semaphore_wait(barrier, N_ROW - 1 + N_GRP - 1 + 2)

    def gather_steps(app, panel):
        def place(b, first, second):
            swap = b % 2
            sign = 1 - 2 * ((b // 2) % 2)
            to_x = (x + 2 * SIDE + sign * (first * (1 - swap) + second * swap)) % SIDE
            to_z = (z + 2 * SIDE + sign * (first * swap + second * (1 - swap))) % SIDE
            return to_x * SIDE + to_z

        def send(b, u, v, first, second):
            slot = place(b, -u, -v) * BLOCKS + b
            to_u, to_v = (u + first) % SIDE, (v + second) % SIDE
            pltpu.make_async_remote_copy(
                src_ref=panel.at[slot],
                dst_ref=panel.at[slot],
                send_sem=send_sem.at[app, b],
                recv_sem=recv_sem.at[app, b, to_u * SIDE + to_v],
                device_id=(place(b, first, second), grp),
                device_id_type=MESH,
            ).start()

        def arrived(b, u, v):
            slot = place(b, -u, -v) * BLOCKS + b
            pltpu.make_async_copy(
                panel.at[slot], panel.at[slot], recv_sem.at[app, b, u * SIDE + v]
            ).wait()

        def send_own(b):
            send(b, 0, 0, 1, 0)
            send(b, 0, 0, -1, 0)
            send(b, 0, 0, 0, 1)
            send(b, 0, 0, 0, -1)

        def forward():
            @pl.loop(0, BLOCKS)
            def _(b):
                arrived(b, 1, 0)
                send(b, 1, 0, 1, 0)
                send(b, 1, 0, 0, 1)
                send(b, 1, 0, 0, -1)
                arrived(b, 3, 0)
                send(b, 3, 0, 0, 1)
                send(b, 3, 0, 0, -1)

            @pl.loop(0, BLOCKS)
            def _(b):
                arrived(b, 2, 0)
                send(b, 2, 0, 0, 1)
                send(b, 2, 0, 0, -1)
                arrived(b, 0, 1)
                send(b, 0, 1, 0, 1)

            @pl.loop(0, BLOCKS)
            def _(b):
                arrived(b, 1, 1)
                send(b, 1, 1, 0, 1)
                arrived(b, 3, 1)
                send(b, 3, 1, 0, 1)

            @pl.loop(0, BLOCKS)
            def _(b):
                arrived(b, 2, 1)
                send(b, 2, 1, 0, 1)

            @pl.loop(0, BLOCKS)
            def _(b):
                for u in range(SIDE):
                    arrived(b, u, 3)
                for u in range(SIDE):
                    arrived(b, u, 2)

        def sent():
            @pl.loop(0, BLOCKS)
            def _(b):
                pltpu.make_async_copy(
                    panel.at[pl.ds(0, N_ROW - 1)],
                    panel.at[pl.ds(0, N_ROW - 1)],
                    send_sem.at[app, b],
                ).wait()

        return send_own, forward, sent

    def halo(app, panel):
        tail = pltpu.make_async_remote_copy(
            src_ref=panel.at[own + BLOCKS - 1],
            dst_ref=panel.at[LEFT],
            send_sem=halo_send.at[app, 0],
            recv_sem=halo_recv.at[app, 0],
            device_id=after_id,
            device_id_type=MESH,
        )
        head = pltpu.make_async_remote_copy(
            src_ref=panel.at[own],
            dst_ref=panel.at[RIGHT],
            send_sem=halo_send.at[app, 1],
            recv_sem=halo_recv.at[app, 1],
            device_id=before_id,
            device_id_type=MESH,
        )
        return head, tail

    def near(panel, i):
        left = jnp.where(i == 0, jnp.where(device == 0, ZERO, LEFT), own + i - 1)
        right = jnp.where(
            i == BLOCKS - 1,
            jnp.where(device == N_ROW * N_GRP - 1, ZERO, RIGHT),
            own + i + 1,
        )
        return (
            dot(band_v[i, 0], panel[left])
            + dot(band_v[i, 1], panel[own + i])
            + dot(band_v[i, 2], panel[right])
        )

    def long_range(panel, i):
        total = acc[i]
        live_slots = count[i]
        for s in range(SLOTS):
            live = (s < live_slots).astype(jnp.int32)
            index = (owner[i, s] * BLOCKS + local[i, s]) * live + ZERO * (1 - live)
            total = total + dot(far_v[i, s], panel[index])
        return total

    send_own, forward, sent_a = gather_steps(0, panel_a)
    head, tail = halo(0, panel_a)
    pl.loop(0, BLOCKS)(send_own)
    head.start()
    tail.start()
    load_band.wait()
    head.wait()
    tail.wait()

    @pl.loop(0, BLOCKS)
    def _(i):
        acc[i] = near(panel_a, i)

    forward()
    load_far.wait()

    send_own, forward, sent_b = gather_steps(1, panel_b)
    head, tail = halo(1, panel_b)

    @pl.loop(0, BLOCKS)
    def _(i):
        panel_b[own + i] = long_range(panel_a, i).astype(BF16)
        send_own(i)

    head.start()
    tail.start()
    head.wait()
    tail.wait()

    @pl.loop(0, BLOCKS)
    def _(i):
        acc[i] = near(panel_b, i)

    forward()

    gram_v[...] = jnp.zeros((B, B), F32)
    gram_c[...] = jnp.zeros((B, B), F32)

    @pl.loop(0, BLOCKS)
    def _(i):
        block = long_range(panel_b, i)
        acc[i] = block
        top = block.astype(BF16)
        rest = block - top.astype(F32)
        middle = rest.astype(BF16)
        low = (rest - middle.astype(F32)).astype(BF16)
        top_t = top.T
        gram_v[...] += dot(top_t, top) + dot(middle.T, middle)
        gram_c[...] += dot(top_t, middle) + dot(top_t, low)

    store = pltpu.make_async_copy(acc, second_out, out_sem.at[0])
    store.start()
    cross = gram_c[...]
    gram_v[...] += cross + cross.T

    def scatter(k):
        to = (row + k) % N_ROW
        return pltpu.make_async_remote_copy(
            src_ref=gram_v.at[pl.ds(to * PART, PART)],
            dst_ref=parts.at[row],
            send_sem=scatter_send.at[k],
            recv_sem=scatter_recv.at[k],
            device_id=(to, grp),
            device_id_type=MESH,
        )

    @pl.loop(1, N_ROW)
    def _(k):
        scatter(k).start()

    parts[row] = gram_v[pl.ds(row * PART, PART)]

    @pl.loop(1, N_ROW)
    def _(k):
        origin = (row + N_ROW - k) % N_ROW
        pltpu.make_async_copy(parts.at[origin], parts.at[origin], scatter_recv.at[k]).wait()

    total = parts[0]
    for k in range(1, N_ROW):
        total = total + parts[k]
    shares[grp] = total

    def share(k):
        return pltpu.make_async_remote_copy(
            src_ref=shares.at[grp],
            dst_ref=shares.at[grp],
            send_sem=share_send.at[k],
            recv_sem=share_recv.at[k],
            device_id=(row, (grp + k) % N_GRP),
            device_id_type=MESH,
        )

    @pl.loop(1, N_GRP)
    def _(k):
        share(k).start()

    @pl.loop(1, N_GRP)
    def _(k):
        origin = (grp + N_GRP - k) % N_GRP
        pltpu.make_async_copy(shares.at[origin], shares.at[origin], share_recv.at[k]).wait()

    total = shares[0]
    for k in range(1, N_GRP):
        total = total + shares[k]
    gram_c[pl.ds(row * PART, PART)] = total

    def spread(k):
        mine = pl.ds(row * PART, PART)
        return pltpu.make_async_remote_copy(
            src_ref=gram_c.at[mine],
            dst_ref=gram_c.at[mine],
            send_sem=spread_send.at[k],
            recv_sem=spread_recv.at[k],
            device_id=((row + k) % N_ROW, grp),
            device_id_type=MESH,
        )

    @pl.loop(1, N_ROW)
    def _(k):
        spread(k).start()

    @pl.loop(1, N_ROW)
    def _(k):
        theirs = pl.ds(((row + N_ROW - k) % N_ROW) * PART, PART)
        pltpu.make_async_copy(gram_c.at[theirs], gram_c.at[theirs], spread_recv.at[k]).wait()

    @pl.loop(1, N_ROW)
    def _(k):
        scatter(k).wait_send()
        spread(k).wait_send()

    @pl.loop(1, N_GRP)
    def _(k):
        share(k).wait_send()

    finish = pltpu.make_async_copy(gram_c, gram_out, out_sem.at[1])
    finish.start()
    sent_a()
    sent_b()
    store.wait()
    finish.wait()


def power_step(sketch, band_tiles, far_tiles, far_owner, far_local, far_count):
    any_space = pl.BlockSpec(memory_space=pl.ANY)
    scalars = pl.BlockSpec(memory_space=pltpu.SMEM)
    dma = pltpu.SemaphoreType.DMA
    return pl.pallas_call(
        range_kernel,
        out_shape=(
            jax.ShapeDtypeStruct((BLOCKS, B, B), F32),
            jax.ShapeDtypeStruct((B, B), F32),
        ),
        in_specs=[any_space, any_space, any_space, scalars, scalars, scalars],
        out_specs=(any_space, any_space),
        scratch_shapes=[
            pltpu.VMEM((N_PANEL + 3, B, B), BF16),
            pltpu.VMEM((N_PANEL + 3, B, B), BF16),
            pltpu.VMEM((BLOCKS, 3, B, B), BF16),
            pltpu.VMEM((BLOCKS, SLOTS, B, B), BF16),
            pltpu.VMEM((BLOCKS, B, B), F32),
            pltpu.VMEM((B, B), F32),
            pltpu.VMEM((B, B), F32),
            pltpu.VMEM((N_ROW, PART, B), F32),
            pltpu.VMEM((N_GRP, PART, B), F32),
            dma((3,)),
            dma((2, BLOCKS, N_ROW)),
            dma((2, BLOCKS)),
            dma((2, 2)),
            dma((2, 2)),
            dma((N_ROW,)),
            dma((N_ROW,)),
            dma((N_GRP,)),
            dma((N_GRP,)),
            dma((N_ROW,)),
            dma((N_ROW,)),
            dma((2,)),
        ],
        compiler_params=pltpu.CompilerParams(
            collective_id=0, has_side_effects=True, vmem_limit_bytes=56 * 1024 * 1024
        ),
        cost_estimate=pl.CostEstimate(
            flops=4 * 88 * B**3, bytes_accessed=15 << 20, transcendentals=0
        ),
    )(sketch, band_tiles, far_tiles, far_owner, far_local, far_count)


def body(sketch, band_tiles, far_tiles, far_owner, far_local, far_count):
    second, gram = power_step(sketch, band_tiles, far_tiles, far_owner, far_local, far_count)
    flat_rows = second.reshape(BLOCKS * B, B)
    lower_factor = jnp.linalg.cholesky(gram)
    solved = jax.scipy.linalg.solve_triangular(lower_factor, flat_rows.T, lower=True)
    scale_rows = math.sqrt(BLOCKS * B * N_ROW * N_GRP)
    basis = (solved.T * scale_rows).reshape(BLOCKS, B, B)
    factor = lower_factor.T / scale_rows
    return (basis, factor)


def solution(mesh):
    in_specs = (
        P(("row", "grp"), None, None),
        P(("row", "grp"), None, None, None),
        P(("row", "grp"), None, None, None),
        P(("row", "grp"), None),
        P(("row", "grp"), None),
        P(("row", "grp")),
    )
    out_specs = (P(("row", "grp"), None, None), P())
    return jax.shard_map(body, mesh=mesh, in_specs=in_specs, out_specs=out_specs, check_vma=False)
```

```python
import functools
import math

import jax
import jax.numpy as jnp
from jax import lax
from jax.experimental import pallas as pl
from jax.experimental.pallas import tpu as pltpu
from jax.sharding import PartitionSpec as P

MESH = pl.DeviceIdType.MESH
SIDE = 4
N_ROW = SIDE * SIDE
N_GRP = 8
BLOCKS = 8
SLOTS = 8
B = 256
N_PANEL = N_ROW * BLOCKS
ZERO, LEFT, RIGHT = N_PANEL, N_PANEL + 1, N_PANEL + 2
PART = B // N_ROW
F32 = jnp.float32
BF16 = jnp.bfloat16
SUB, LANE = 8, 128
SCALE = math.sqrt(BLOCKS * B * N_ROW * N_GRP)


def dot(a, b):
    return jnp.dot(a, b, preferred_element_type=F32)


def range_kernel(
    sketch, band, far, owner, local, count,
    second_out, gram_out,
    panel_a, panel_b, band_v, far_v, acc, gram_v, gram_c, parts, shares,
    load_sem, recv_sem, send_sem, halo_send, halo_recv,
    scatter_send, scatter_recv, share_send, share_recv, spread_send, spread_recv, out_sem,
):
    row, grp = lax.axis_index("row"), lax.axis_index("grp")
    x, z = row // SIDE, row % SIDE
    device = row * N_GRP + grp
    after, before = (device + 1) % (N_ROW * N_GRP), (device + N_ROW * N_GRP - 1) % (N_ROW * N_GRP)
    after_id = (after // N_GRP, after % N_GRP)
    before_id = (before // N_GRP, before % N_GRP)
    own = row * BLOCKS

    load_panel = pltpu.make_async_copy(sketch, panel_a.at[pl.ds(own, BLOCKS)], load_sem.at[0])
    load_band = pltpu.make_async_copy(band, band_v, load_sem.at[1])
    load_far = pltpu.make_async_copy(far, far_v, load_sem.at[2])
    load_panel.start()
    load_band.start()
    load_far.start()

    barrier = pltpu.get_barrier_semaphore()

    def greet(device_id):
        pl.semaphore_signal(barrier, inc=1, device_id=device_id, device_id_type=MESH)

    @pl.loop(1, N_ROW)
    def _(k):
        greet(((row + k) % N_ROW, grp))

    @pl.loop(1, N_GRP)
    def _(k):
        greet((row, (grp + k) % N_GRP))

    greet(after_id)
    greet(before_id)
    for panel in (panel_a, panel_b):
        panel[ZERO] = jnp.zeros((B, B), BF16)
    load_panel.wait()
    pl.semaphore_wait(barrier, N_ROW - 1 + N_GRP - 1 + 2)

    def gather_steps(app, panel):
        def place(b, first, second):
            swap = b % 2
            sign = 1 - 2 * ((b // 2) % 2)
            to_x = (x + 2 * SIDE + sign * (first * (1 - swap) + second * swap)) % SIDE
            to_z = (z + 2 * SIDE + sign * (first * swap + second * (1 - swap))) % SIDE
            return to_x * SIDE + to_z

        def send(b, u, v, first, second):
            slot = place(b, -u, -v) * BLOCKS + b
            to_u, to_v = (u + first) % SIDE, (v + second) % SIDE
            pltpu.make_async_remote_copy(
                src_ref=panel.at[slot],
                dst_ref=panel.at[slot],
                send_sem=send_sem.at[app, b],
                recv_sem=recv_sem.at[app, b, to_u * SIDE + to_v],
                device_id=(place(b, first, second), grp),
                device_id_type=MESH,
            ).start()

        def arrived(b, u, v):
            slot = place(b, -u, -v) * BLOCKS + b
            pltpu.make_async_copy(
                panel.at[slot], panel.at[slot], recv_sem.at[app, b, u * SIDE + v]
            ).wait()

        def send_own(b):
            send(b, 0, 0, 1, 0)
            send(b, 0, 0, -1, 0)
            send(b, 0, 0, 0, 1)
            send(b, 0, 0, 0, -1)

        def forward():
            @pl.loop(0, BLOCKS)
            def _(b):
                arrived(b, 1, 0)
                send(b, 1, 0, 1, 0)
                send(b, 1, 0, 0, 1)
                send(b, 1, 0, 0, -1)
                arrived(b, 3, 0)
                send(b, 3, 0, 0, 1)
                send(b, 3, 0, 0, -1)

            @pl.loop(0, BLOCKS)
            def _(b):
                arrived(b, 2, 0)
                send(b, 2, 0, 0, 1)
                send(b, 2, 0, 0, -1)
                arrived(b, 0, 1)
                send(b, 0, 1, 0, 1)

            @pl.loop(0, BLOCKS)
            def _(b):
                arrived(b, 1, 1)
                send(b, 1, 1, 0, 1)
                arrived(b, 3, 1)
                send(b, 3, 1, 0, 1)

            @pl.loop(0, BLOCKS)
            def _(b):
                arrived(b, 2, 1)
                send(b, 2, 1, 0, 1)

            @pl.loop(0, BLOCKS)
            def _(b):
                for u in range(SIDE):
                    arrived(b, u, 3)
                for u in range(SIDE):
                    arrived(b, u, 2)

        def sent():
            @pl.loop(0, BLOCKS)
            def _(b):
                pltpu.make_async_copy(
                    panel.at[pl.ds(0, N_ROW - 1)],
                    panel.at[pl.ds(0, N_ROW - 1)],
                    send_sem.at[app, b],
                ).wait()

        return send_own, forward, sent

    def halo(app, panel):
        tail = pltpu.make_async_remote_copy(
            src_ref=panel.at[own + BLOCKS - 1],
            dst_ref=panel.at[LEFT],
            send_sem=halo_send.at[app, 0],
            recv_sem=halo_recv.at[app, 0],
            device_id=after_id,
            device_id_type=MESH,
        )
        head = pltpu.make_async_remote_copy(
            src_ref=panel.at[own],
            dst_ref=panel.at[RIGHT],
            send_sem=halo_send.at[app, 1],
            recv_sem=halo_recv.at[app, 1],
            device_id=before_id,
            device_id_type=MESH,
        )
        return head, tail

    def near(panel, i):
        left = jnp.where(i == 0, jnp.where(device == 0, ZERO, LEFT), own + i - 1)
        right = jnp.where(
            i == BLOCKS - 1,
            jnp.where(device == N_ROW * N_GRP - 1, ZERO, RIGHT),
            own + i + 1,
        )
        return (
            dot(band_v[i, 0], panel[left])
            + dot(band_v[i, 1], panel[own + i])
            + dot(band_v[i, 2], panel[right])
        )

    def long_range(panel, i):
        total = acc[i]
        live_slots = count[i]
        for s in range(SLOTS):
            live = (s < live_slots).astype(jnp.int32)
            index = (owner[i, s] * BLOCKS + local[i, s]) * live + ZERO * (1 - live)
            total = total + dot(far_v[i, s], panel[index])
        return total

    send_own, forward, sent_a = gather_steps(0, panel_a)
    head, tail = halo(0, panel_a)
    pl.loop(0, BLOCKS)(send_own)
    head.start()
    tail.start()
    load_band.wait()
    head.wait()
    tail.wait()

    @pl.loop(0, BLOCKS)
    def _(i):
        acc[i] = near(panel_a, i)

    forward()
    load_far.wait()

    send_own, forward, sent_b = gather_steps(1, panel_b)
    head, tail = halo(1, panel_b)

    @pl.loop(0, BLOCKS)
    def _(i):
        panel_b[own + i] = long_range(panel_a, i).astype(BF16)
        send_own(i)

    head.start()
    tail.start()
    head.wait()
    tail.wait()

    @pl.loop(0, BLOCKS)
    def _(i):
        acc[i] = near(panel_b, i)

    forward()

    gram_v[...] = jnp.zeros((B, B), F32)
    gram_c[...] = jnp.zeros((B, B), F32)

    @pl.loop(0, BLOCKS)
    def _(i):
        block = long_range(panel_b, i)
        acc[i] = block
        top = block.astype(BF16)
        rest = block - top.astype(F32)
        middle = rest.astype(BF16)
        low = (rest - middle.astype(F32)).astype(BF16)
        top_t = top.T
        gram_v[...] += dot(top_t, top) + dot(middle.T, middle)
        gram_c[...] += dot(top_t, middle) + dot(top_t, low)

    store = pltpu.make_async_copy(acc, second_out, out_sem.at[0])
    store.start()
    cross = gram_c[...]
    gram_v[...] += cross + cross.T

    def scatter(k):
        to = (row + k) % N_ROW
        return pltpu.make_async_remote_copy(
            src_ref=gram_v.at[pl.ds(to * PART, PART)],
            dst_ref=parts.at[row],
            send_sem=scatter_send.at[k],
            recv_sem=scatter_recv.at[k],
            device_id=(to, grp),
            device_id_type=MESH,
        )

    @pl.loop(1, N_ROW)
    def _(k):
        scatter(k).start()

    parts[row] = gram_v[pl.ds(row * PART, PART)]

    @pl.loop(1, N_ROW)
    def _(k):
        origin = (row + N_ROW - k) % N_ROW
        pltpu.make_async_copy(parts.at[origin], parts.at[origin], scatter_recv.at[k]).wait()

    total = parts[0]
    for k in range(1, N_ROW):
        total = total + parts[k]
    shares[grp] = total

    def share(k):
        return pltpu.make_async_remote_copy(
            src_ref=shares.at[grp],
            dst_ref=shares.at[grp],
            send_sem=share_send.at[k],
            recv_sem=share_recv.at[k],
            device_id=(row, (grp + k) % N_GRP),
            device_id_type=MESH,
        )

    @pl.loop(1, N_GRP)
    def _(k):
        share(k).start()

    @pl.loop(1, N_GRP)
    def _(k):
        origin = (grp + N_GRP - k) % N_GRP
        pltpu.make_async_copy(shares.at[origin], shares.at[origin], share_recv.at[k]).wait()

    total = shares[0]
    for k in range(1, N_GRP):
        total = total + shares[k]
    gram_c[pl.ds(row * PART, PART)] = total

    def spread(k):
        mine = pl.ds(row * PART, PART)
        return pltpu.make_async_remote_copy(
            src_ref=gram_c.at[mine],
            dst_ref=gram_c.at[mine],
            send_sem=spread_send.at[k],
            recv_sem=spread_recv.at[k],
            device_id=((row + k) % N_ROW, grp),
            device_id_type=MESH,
        )

    @pl.loop(1, N_ROW)
    def _(k):
        spread(k).start()

    @pl.loop(1, N_ROW)
    def _(k):
        theirs = pl.ds(((row + N_ROW - k) % N_ROW) * PART, PART)
        pltpu.make_async_copy(gram_c.at[theirs], gram_c.at[theirs], spread_recv.at[k]).wait()

    @pl.loop(1, N_ROW)
    def _(k):
        scatter(k).wait_send()
        spread(k).wait_send()

    @pl.loop(1, N_GRP)
    def _(k):
        share(k).wait_send()

    finish = pltpu.make_async_copy(gram_c, gram_out, out_sem.at[1])
    finish.start()
    sent_a()
    sent_b()
    store.wait()
    finish.wait()


def factor_kernel(gram, second, basis, factor, m, inv_v, second_v, out_v, sem):
    load = pltpu.make_async_copy(second, second_v, sem.at[0])
    load.start()
    tile = (SUB, LANE)
    halves = range(B // LANE)
    lanes = lax.broadcasted_iota(jnp.int32, tile, 1)
    subs = lax.broadcasted_iota(jnp.int32, tile, 0)
    m[...] = gram[...]

    def row_of(a, r):
        return jnp.broadcast_to(a[r : r + 1, :], tile)

    def column_of(a, c):
        return jnp.broadcast_to(a[:, c : c + 1], tile)

    def at(i, l):
        return (pl.ds(i * SUB, SUB), pl.ds(l * LANE, LANE))

    for g in range(B // SUB):
        home, first = g * SUB // LANE, g * SUB % LANE
        inside = (lanes >= first) & (lanes < first + SUB)
        pivot = [m[at(g, l)] for l in halves]
        columns = [column_of(pivot[home], first + c) for c in range(SUB)]
        s = {(r, c): row_of(columns[c], r) for c in range(SUB) for r in range(c, SUB)}
        roots, ratios = [], {}
        for j in range(SUB):
            d = s[j, j]
            inverse = 1.0 / d
            roots.append(lax.rsqrt(d))
            old = {r: s[max(r, j), min(r, j)] for r in range(SUB) if r != j}
            new = {r: old[r] * inverse for r in old}
            for r in old:
                for c in old:
                    if c <= r:
                        s[r, c] = s[r, c] - old[r] * new[c]
            for r in old:
                s[max(r, j), min(r, j)] = new[r]
                if r > j:
                    ratios[r, j] = new[r]
            s[j, j] = -inverse
        unit = jnp.where(inside, (lanes - first == subs).astype(F32), pivot[home])
        source = [unit if l == home else pivot[l] for l in halves]
        rows = [[row_of(source[l], r) for l in halves] for r in range(SUB)]
        weights = []
        for c in range(SUB):
            per = []
            for l in halves:
                terms = [s[max(r, c), min(r, c)] * rows[r][l] for r in range(SUB)]
                while len(terms) > 1:
                    terms = [terms[k] + terms[k + 1] for k in range(0, len(terms), 2)]
                per.append(terms[0])
            weights.append(per)
        for i in range(g + 1, B // SUB):
            left = m[at(i, home)]
            columns = [column_of(left, first + c) for c in range(SUB)]
            for l in halves:
                value = jnp.where(inside, 0.0, left) if l == home else m[at(i, l)]
                terms = [columns[c] * weights[c][l] for c in range(SUB)]
                while len(terms) > 1:
                    terms = [terms[k] + terms[k + 1] for k in range(0, len(terms), 2)]
                m[at(i, l)] = value + terms[0]
        upper = [row_of(pivot[home], r) for r in range(SUB)]
        inv_tiles = [jnp.zeros(tile, F32) for _ in halves]
        fac_tiles = [jnp.zeros(tile, F32) for _ in halves]
        for r in range(SUB):
            for j in range(r):
                upper[r] = upper[r] - ratios[r, j] * upper[j]
                for l in halves:
                    rows[r][l] = rows[r][l] - ratios[r, j] * rows[j][l]
            here = subs == r
            for l in halves:
                if l <= home:
                    inv_tiles[l] = jnp.where(here, rows[r][l] * roots[r], inv_tiles[l])
                if l > home:
                    fac_tiles[l] = jnp.where(here, rows[r][l] * roots[r], fac_tiles[l])
                if l == home:
                    fac_tiles[l] = jnp.where(here, upper[r] * roots[r], fac_tiles[l])
        inv_tiles[home] = jnp.where(lanes < first + SUB, inv_tiles[home], 0.0)
        fac_tiles[home] = jnp.where(lanes - first >= subs, fac_tiles[home], 0.0)
        for l in halves:
            inv_v[at(g, l)] = inv_tiles[l] * SCALE
            factor[at(g, l)] = fac_tiles[l] * (1.0 / SCALE)

    turned = inv_v[...].T
    top = turned.astype(BF16)
    rest = (turned - top.astype(F32)).astype(BF16)
    load.wait()

    def store(i):
        return pltpu.make_async_copy(out_v.at[i], basis.at[i], sem.at[1 + i])

    @pl.loop(0, BLOCKS)
    def _(i):
        x = second_v[i]
        x_top = x.astype(BF16)
        x_rest = (x - x_top.astype(F32)).astype(BF16)
        out_v[i] = dot(x_top, top) + (dot(x_top, rest) + dot(x_rest, top))
        store(i).start()

    @pl.loop(0, BLOCKS)
    def _(i):
        store(i).wait()


def power_step(sketch, band_tiles, far_tiles, far_owner, far_local, far_count):
    any_space = pl.BlockSpec(memory_space=pl.ANY)
    scalars = pl.BlockSpec(memory_space=pltpu.SMEM)
    dma = pltpu.SemaphoreType.DMA
    return pl.pallas_call(
        range_kernel,
        out_shape=(
            jax.ShapeDtypeStruct((BLOCKS, B, B), F32),
            jax.ShapeDtypeStruct((B, B), F32),
        ),
        in_specs=[any_space, any_space, any_space, scalars, scalars, scalars],
        out_specs=(any_space, any_space),
        scratch_shapes=[
            pltpu.VMEM((N_PANEL + 3, B, B), BF16),
            pltpu.VMEM((N_PANEL + 3, B, B), BF16),
            pltpu.VMEM((BLOCKS, 3, B, B), BF16),
            pltpu.VMEM((BLOCKS, SLOTS, B, B), BF16),
            pltpu.VMEM((BLOCKS, B, B), F32),
            pltpu.VMEM((B, B), F32),
            pltpu.VMEM((B, B), F32),
            pltpu.VMEM((N_ROW, PART, B), F32),
            pltpu.VMEM((N_GRP, PART, B), F32),
            dma((3,)),
            dma((2, BLOCKS, N_ROW)),
            dma((2, BLOCKS)),
            dma((2, 2)),
            dma((2, 2)),
            dma((N_ROW,)),
            dma((N_ROW,)),
            dma((N_GRP,)),
            dma((N_GRP,)),
            dma((N_ROW,)),
            dma((N_ROW,)),
            dma((2,)),
        ],
        compiler_params=pltpu.CompilerParams(
            collective_id=0, has_side_effects=True, vmem_limit_bytes=56 * 1024 * 1024
        ),
        cost_estimate=pl.CostEstimate(
            flops=4 * 88 * B**3, bytes_accessed=15 << 20, transcendentals=0
        ),
    )(sketch, band_tiles, far_tiles, far_owner, far_local, far_count)


def orthonormalize(gram, second):
    whole = pl.BlockSpec(memory_space=pltpu.VMEM)
    any_space = pl.BlockSpec(memory_space=pl.ANY)
    return pl.pallas_call(
        factor_kernel,
        out_shape=(
            jax.ShapeDtypeStruct((BLOCKS, B, B), F32),
            jax.ShapeDtypeStruct((B, B), F32),
        ),
        in_specs=[whole, any_space],
        out_specs=(any_space, whole),
        scratch_shapes=[
            pltpu.VMEM((B, B), F32),
            pltpu.VMEM((B, B), F32),
            pltpu.VMEM((BLOCKS, B, B), F32),
            pltpu.VMEM((BLOCKS, B, B), F32),
            pltpu.SemaphoreType.DMA((1 + BLOCKS,)),
        ],
        compiler_params=pltpu.CompilerParams(vmem_limit_bytes=32 * 1024 * 1024),
    )(gram, second)


def body(sketch, band_tiles, far_tiles, far_owner, far_local, far_count):
    second, gram = power_step(sketch, band_tiles, far_tiles, far_owner, far_local, far_count)
    return orthonormalize(gram, second)


def solution(mesh):
    in_specs = (
        P(("row", "grp"), None, None),
        P(("row", "grp"), None, None, None),
        P(("row", "grp"), None, None, None),
        P(("row", "grp"), None),
        P(("row", "grp"), None),
        P(("row", "grp")),
    )
    out_specs = (P(("row", "grp"), None, None), P())
    return jax.shard_map(body, mesh=mesh, in_specs=in_specs, out_specs=out_specs, check_vma=False)
```

```python
import math

import jax
import jax.numpy as jnp
from jax import lax
from jax.experimental import pallas as pl
from jax.experimental.pallas import tpu as pltpu
from jax.sharding import PartitionSpec as P

MESH = pl.DeviceIdType.MESH
SIDE = 4
N_ROW = SIDE * SIDE
N_GRP = 8
BLOCKS = 8
SLOTS = 8
B = 256
N_PANEL = N_ROW * BLOCKS
ZERO, LEFT, RIGHT = N_PANEL, N_PANEL + 1, N_PANEL + 2
PART = B // N_ROW
CAP = 6
QUARTERS = 4
UNITS = 8
TALL, WIDE = B // 4, B // 2
F32 = jnp.float32
BF16 = jnp.bfloat16
SUB, LANE = 8, 128
SCALE = math.sqrt(BLOCKS * B * N_ROW * N_GRP)


def dot(a, b):
    return jnp.dot(a, b, preferred_element_type=F32)


def range_kernel(
    sketch, band, far, owner, local, count,
    second_out, gram_out,
    panel_a, panel_b, band_v, far_v, acc, packed, gram_v, gram_c, parts, shares,
    wants_v, wants_in, index_v, wants_s, index_s,
    load_sem, recv_sem, send_sem, halo_send, halo_recv, wants_send, wants_recv, table_sem,
    scatter_send, scatter_recv, share_send, share_recv, spread_send, spread_recv, out_sem,
):
    row, grp = lax.axis_index("row"), lax.axis_index("grp")
    x, z = row // SIDE, row % SIDE
    device = row * N_GRP + grp
    after, before = (device + 1) % (N_ROW * N_GRP), (device + N_ROW * N_GRP - 1) % (N_ROW * N_GRP)
    after_id = (after // N_GRP, after % N_GRP)
    before_id = (before // N_GRP, before % N_GRP)
    own = row * BLOCKS

    def load_unit(n):
        h, q = n // QUARTERS, n % QUARTERS
        return pltpu.make_async_copy(
            sketch.at[:, pl.ds(q * TALL, TALL), pl.ds(h * WIDE, WIDE)],
            panel_a.at[n, pl.ds(own, BLOCKS)],
            load_sem.at[2 + n],
        )

    load_band = pltpu.make_async_copy(band, band_v, load_sem.at[0])
    load_far = pltpu.make_async_copy(far, far_v, load_sem.at[1])
    for n in range(UNITS):
        load_unit(n).start()
    load_band.start()
    load_far.start()

    barrier = pltpu.get_barrier_semaphore()

    def greet(device_id):
        pl.semaphore_signal(barrier, inc=1, device_id=device_id, device_id_type=MESH)

    @pl.loop(1, N_ROW)
    def _(k):
        greet(((row + k) % N_ROW, grp))

    @pl.loop(1, N_GRP)
    def _(k):
        greet((row, (grp + k) % N_GRP))

    greet(after_id)
    greet(before_id)

    table = (8, 128)
    lanes = lax.broadcasted_iota(jnp.int32, table, 1)
    subs = lax.broadcasted_iota(jnp.int32, table, 0)
    nothing = jnp.zeros(table, jnp.int32)

    def spread_entry(e, carry):
        owners, locals_, counts = carry
        i, s = e // SLOTS, e % SLOTS
        here = lanes == e
        return (
            jnp.where(here, owner[i, s], owners),
            jnp.where(here, local[i, s], locals_),
            jnp.where(here, count[i], counts),
        )

    owners, locals_, counts = lax.fori_loop(
        0, BLOCKS * SLOTS, spread_entry, (nothing, nothing, nothing)
    )

    def rank_entry(e, carry):
        wants, seen, ranks = carry
        i, s = e // SLOTS, e % SLOTS
        name = owner[i, s]
        hit = (lanes // SLOTS) == name
        wants = jnp.where(hit & (seen == lanes % SLOTS), local[i, s], wants)
        seen = seen + hit.astype(jnp.int32)
        ranks = ranks + ((owners == name) & (lanes > e)).astype(jnp.int32)
        return wants, seen, ranks

    wants, _, ranks = lax.fori_loop(
        0, BLOCKS * SLOTS, rank_entry, (nothing, nothing, nothing)
    )
    wants_v[...] = wants
    from_x = (x - owners // SIDE + SIDE) % SIDE
    from_z = (z - owners % SIDE + SIDE) % SIDE
    index = nothing
    for q in range(QUARTERS):
        away = from_z if q % 2 == 0 else from_x
        if q // 2 == 1:
            away = (SIDE - away) % SIDE
        leaf = away // 2
        at = owners * BLOCKS + locals_ + leaf * (ranks - locals_)
        at = jnp.where(lanes % SLOTS < counts, at, ZERO)
        index = jnp.where(subs == q, at, index)
    index_v[...] = index
    index_copy = pltpu.make_async_copy(index_v, index_s, table_sem.at[0])
    index_copy.start()

    for panel in (panel_a, panel_b):
        panel[:, ZERO] = jnp.zeros((UNITS, TALL, WIDE), BF16)
    for n in range(UNITS):
        load_unit(n).wait()
    pl.semaphore_wait(barrier, N_ROW - 1 + N_GRP - 1 + 2)

    around = (
        ((x + 1) % SIDE * SIDE + z, 1),
        ((x + SIDE - 1) % SIDE * SIDE + z, 0),
        (x * SIDE + (z + 1) % SIDE, 3),
        (x * SIDE + (z + SIDE - 1) % SIDE, 2),
    )
    tell = [
        pltpu.make_async_remote_copy(
            src_ref=wants_v,
            dst_ref=wants_in.at[side],
            send_sem=wants_send.at[side],
            recv_sem=wants_recv.at[side],
            device_id=(neighbour, grp),
            device_id_type=MESH,
        )
        for neighbour, side in around
    ]
    for one in tell:
        one.start()

    def gather_steps(app, panel):
        def turn(n):
            return n % 2, 1 - 2 * ((n // 2) % 2)

        def place(n, first, second):
            swap, sign = turn(n)
            to_x = (x + 2 * SIDE + sign * (first * (1 - swap) + second * swap)) % SIDE
            to_z = (z + 2 * SIDE + sign * (first * swap + second * (1 - swap))) % SIDE
            return to_x * SIDE + to_z

        def send(n, u, v, first, second):
            slots = pl.ds(place(n, -u, -v) * BLOCKS, BLOCKS)
            to_u, to_v = (u + first) % SIDE, (v + second) % SIDE
            pltpu.make_async_remote_copy(
                src_ref=panel.at[n, slots],
                dst_ref=panel.at[n, slots],
                send_sem=send_sem.at[app, n],
                recv_sem=recv_sem.at[app, n, to_u * SIDE + to_v],
                device_id=(place(n, first, second), grp),
                device_id_type=MESH,
            ).start()

        def send_leaf(n, u, v, second):
            swap, sign = turn(n)
            side = 2 * (1 - swap) + (1 - second * sign) // 2
            source = place(n, -u, -v)
            to_v = (v + second) % SIDE
            leaf = u * 2 + to_v - 2
            blocks = [panel[n, source * BLOCKS + b] for b in range(BLOCKS)]
            for k in range(CAP):
                wanted = wants_s[side, 0, source * SLOTS + k]
                out = blocks[0]
                for b in range(1, BLOCKS):
                    out = jnp.where(wanted == b, blocks[b], out)
                packed[n, leaf, k] = out
            pltpu.make_async_remote_copy(
                src_ref=packed.at[n, leaf],
                dst_ref=panel.at[n, pl.ds(source * BLOCKS, CAP)],
                send_sem=send_sem.at[app, n],
                recv_sem=recv_sem.at[app, n, u * SIDE + to_v],
                device_id=(place(n, 0, second), grp),
                device_id_type=MESH,
            ).start()

        def arrived(n, u, v):
            slots = pl.ds(place(n, -u, -v) * BLOCKS, CAP if v >= 2 else BLOCKS)
            pltpu.make_async_copy(
                panel.at[n, slots], panel.at[n, slots], recv_sem.at[app, n, u * SIDE + v]
            ).wait()

        def send_own(n):
            send(n, 0, 0, 1, 0)
            send(n, 0, 0, -1, 0)
            send(n, 0, 0, 0, 1)

        def forward():
            @pl.loop(0, UNITS)
            def _(n):
                send_leaf(n, 0, 0, -1)

            @pl.loop(0, UNITS)
            def _(n):
                arrived(n, 1, 0)
                send(n, 1, 0, 1, 0)
                send(n, 1, 0, 0, 1)
                send_leaf(n, 1, 0, -1)
                arrived(n, 3, 0)
                send(n, 3, 0, 0, 1)
                send_leaf(n, 3, 0, -1)

            @pl.loop(0, UNITS)
            def _(n):
                arrived(n, 2, 0)
                send(n, 2, 0, 0, 1)
                send_leaf(n, 2, 0, -1)
                arrived(n, 0, 1)
                send_leaf(n, 0, 1, 1)

            @pl.loop(0, UNITS)
            def _(n):
                arrived(n, 1, 1)
                send_leaf(n, 1, 1, 1)
                arrived(n, 3, 1)
                send_leaf(n, 3, 1, 1)

            @pl.loop(0, UNITS)
            def _(n):
                arrived(n, 2, 1)
                send_leaf(n, 2, 1, 1)

            @pl.loop(0, UNITS)
            def _(n):
                for u in range(SIDE):
                    arrived(n, u, 3)
                for u in range(SIDE):
                    arrived(n, u, 2)

        def clear():
            @pl.loop(0, UNITS)
            def _(n):
                for u in range(SIDE):
                    for v in (2, 3):
                        for k in range(CAP, BLOCKS):
                            panel[n, place(n, -u, -v) * BLOCKS + k] = jnp.zeros((TALL, WIDE), BF16)

        def sent():
            total = 7 * BLOCKS + 8 * CAP

            @pl.loop(0, UNITS)
            def _(n):
                pltpu.make_async_copy(
                    panel.at[n, pl.ds(0, total)],
                    panel.at[n, pl.ds(0, total)],
                    send_sem.at[app, n],
                ).wait()

        return send_own, forward, sent, clear

    def halo(app, panel, h):
        units = pl.ds(h * QUARTERS, QUARTERS)
        tail = pltpu.make_async_remote_copy(
            src_ref=panel.at[units, own + BLOCKS - 1],
            dst_ref=panel.at[units, LEFT],
            send_sem=halo_send.at[app, 2 * h],
            recv_sem=halo_recv.at[app, 2 * h],
            device_id=after_id,
            device_id_type=MESH,
        )
        head = pltpu.make_async_remote_copy(
            src_ref=panel.at[units, own],
            dst_ref=panel.at[units, RIGHT],
            send_sem=halo_send.at[app, 2 * h + 1],
            recv_sem=halo_recv.at[app, 2 * h + 1],
            device_id=before_id,
            device_id_type=MESH,
        )
        return head, tail

    def column(panel, h, at):
        return jnp.concatenate(
            [panel[h * QUARTERS + q, at(q)] for q in range(QUARTERS)], axis=0
        )

    def block_of(panel, halves, at):
        return jnp.concatenate([column(panel, h, at) for h in halves], axis=1)

    def near(panel, i, halves):
        left = jnp.where(i == 0, jnp.where(device == 0, ZERO, LEFT), own + i - 1)
        right = jnp.where(
            i == BLOCKS - 1,
            jnp.where(device == N_ROW * N_GRP - 1, ZERO, RIGHT),
            own + i + 1,
        )
        return (
            dot(band_v[i, 0], block_of(panel, halves, lambda q: left))
            + dot(band_v[i, 1], block_of(panel, halves, lambda q: own + i))
            + dot(band_v[i, 2], block_of(panel, halves, lambda q: right))
        )

    def long_range(panel, i, halves, total):
        for s in range(SLOTS):
            remote = block_of(panel, halves, lambda q: index_s[q, i * SLOTS + s])
            total = total + dot(far_v[i, s], remote)
        return total

    both = (0, 1)
    send_own, forward, sent_a, clear = gather_steps(0, panel_a)
    pl.loop(0, UNITS)(send_own)
    edges = [copy for h in both for copy in halo(0, panel_a, h)]
    for copy in edges:
        copy.start()
    clear()
    for one in tell:
        one.wait()
    wants_copy = pltpu.make_async_copy(wants_in, wants_s, table_sem.at[1])
    wants_copy.start()
    wants_copy.wait()
    index_copy.wait()
    forward()
    load_band.wait()
    load_far.wait()
    for copy in edges:
        copy.wait()

    send_own, forward, sent_b, clear = gather_steps(1, panel_b)
    edges = []
    for h in both:

        @pl.loop(0, BLOCKS)
        def _(i):
            total = long_range(panel_a, i, (h,), near(panel_a, i, (h,)))
            value = total.astype(BF16)
            for q in range(QUARTERS):
                panel_b[h * QUARTERS + q, own + i] = value[q * TALL : (q + 1) * TALL]

        pl.loop(h * QUARTERS, (h + 1) * QUARTERS)(send_own)
        edges += halo(1, panel_b, h)
        for copy in edges[-2:]:
            copy.start()

    sent_a()
    clear()
    forward()
    for copy in edges:
        copy.wait()

    gram_v[...] = jnp.zeros((B, B), F32)
    gram_c[...] = jnp.zeros((B, B), F32)

    @pl.loop(0, BLOCKS)
    def _(i):
        block = long_range(panel_b, i, both, near(panel_b, i, both))
        acc[i] = block
        top = block.astype(BF16)
        rest = block - top.astype(F32)
        middle = rest.astype(BF16)
        low = (rest - middle.astype(F32)).astype(BF16)
        top_t = top.T
        gram_v[...] += dot(top_t, top) + dot(middle.T, middle)
        gram_c[...] += dot(top_t, middle) + dot(top_t, low)

    store = pltpu.make_async_copy(acc, second_out, out_sem.at[0])
    store.start()
    cross = gram_c[...]
    gram_v[...] += cross + cross.T

    def scatter(k):
        to = (row + k) % N_ROW
        return pltpu.make_async_remote_copy(
            src_ref=gram_v.at[pl.ds(to * PART, PART)],
            dst_ref=parts.at[row],
            send_sem=scatter_send.at[k],
            recv_sem=scatter_recv.at[k],
            device_id=(to, grp),
            device_id_type=MESH,
        )

    @pl.loop(1, N_ROW)
    def _(k):
        scatter(k).start()

    parts[row] = gram_v[pl.ds(row * PART, PART)]

    @pl.loop(1, N_ROW)
    def _(k):
        origin = (row + N_ROW - k) % N_ROW
        pltpu.make_async_copy(parts.at[origin], parts.at[origin], scatter_recv.at[k]).wait()

    total = parts[0]
    for k in range(1, N_ROW):
        total = total + parts[k]
    shares[grp] = total

    def share(k):
        return pltpu.make_async_remote_copy(
            src_ref=shares.at[grp],
            dst_ref=shares.at[grp],
            send_sem=share_send.at[k],
            recv_sem=share_recv.at[k],
            device_id=(row, (grp + k) % N_GRP),
            device_id_type=MESH,
        )

    @pl.loop(1, N_GRP)
    def _(k):
        share(k).start()

    @pl.loop(1, N_GRP)
    def _(k):
        origin = (grp + N_GRP - k) % N_GRP
        pltpu.make_async_copy(shares.at[origin], shares.at[origin], share_recv.at[k]).wait()

    total = shares[0]
    for k in range(1, N_GRP):
        total = total + shares[k]
    gram_c[pl.ds(row * PART, PART)] = total

    def spread(k):
        mine = pl.ds(row * PART, PART)
        return pltpu.make_async_remote_copy(
            src_ref=gram_c.at[mine],
            dst_ref=gram_c.at[mine],
            send_sem=spread_send.at[k],
            recv_sem=spread_recv.at[k],
            device_id=((row + k) % N_ROW, grp),
            device_id_type=MESH,
        )

    @pl.loop(1, N_ROW)
    def _(k):
        spread(k).start()

    @pl.loop(1, N_ROW)
    def _(k):
        theirs = pl.ds(((row + N_ROW - k) % N_ROW) * PART, PART)
        pltpu.make_async_copy(gram_c.at[theirs], gram_c.at[theirs], spread_recv.at[k]).wait()

    @pl.loop(1, N_ROW)
    def _(k):
        scatter(k).wait_send()
        spread(k).wait_send()

    @pl.loop(1, N_GRP)
    def _(k):
        share(k).wait_send()

    finish = pltpu.make_async_copy(gram_c, gram_out, out_sem.at[1])
    finish.start()
    sent_b()
    store.wait()
    finish.wait()


def factor_kernel(gram, second, basis, factor, m, inv_v, second_v, out_v, sem):
    load = pltpu.make_async_copy(second, second_v, sem.at[0])
    load.start()
    tile = (SUB, LANE)
    halves = range(B // LANE)
    lanes = lax.broadcasted_iota(jnp.int32, tile, 1)
    subs = lax.broadcasted_iota(jnp.int32, tile, 0)
    m[...] = gram[...]

    def row_of(a, r):
        return jnp.broadcast_to(a[r : r + 1, :], tile)

    def column_of(a, c):
        return jnp.broadcast_to(a[:, c : c + 1], tile)

    def at(i, l):
        return (pl.ds(i * SUB, SUB), pl.ds(l * LANE, LANE))

    for g in range(B // SUB):
        home, first = g * SUB // LANE, g * SUB % LANE
        inside = (lanes >= first) & (lanes < first + SUB)
        pivot = [m[at(g, l)] for l in halves]
        columns = [column_of(pivot[home], first + c) for c in range(SUB)]
        s = {(r, c): row_of(columns[c], r) for c in range(SUB) for r in range(c, SUB)}
        roots, ratios = [], {}
        for j in range(SUB):
            d = s[j, j]
            inverse = 1.0 / d
            roots.append(lax.rsqrt(d))
            old = {r: s[max(r, j), min(r, j)] for r in range(SUB) if r != j}
            new = {r: old[r] * inverse for r in old}
            for r in old:
                for c in old:
                    if c <= r:
                        s[r, c] = s[r, c] - old[r] * new[c]
            for r in old:
                s[max(r, j), min(r, j)] = new[r]
                if r > j:
                    ratios[r, j] = new[r]
            s[j, j] = -inverse
        unit = jnp.where(inside, (lanes - first == subs).astype(F32), pivot[home])
        source = [unit if l == home else pivot[l] for l in halves]
        rows = [[row_of(source[l], r) for l in halves] for r in range(SUB)]
        weights = []
        for c in range(SUB):
            per = []
            for l in halves:
                terms = [s[max(r, c), min(r, c)] * rows[r][l] for r in range(SUB)]
                while len(terms) > 1:
                    terms = [terms[k] + terms[k + 1] for k in range(0, len(terms), 2)]
                per.append(terms[0])
            weights.append(per)
        for i in range(g + 1, B // SUB):
            left = m[at(i, home)]
            columns = [column_of(left, first + c) for c in range(SUB)]
            for l in halves:
                value = jnp.where(inside, 0.0, left) if l == home else m[at(i, l)]
                terms = [columns[c] * weights[c][l] for c in range(SUB)]
                while len(terms) > 1:
                    terms = [terms[k] + terms[k + 1] for k in range(0, len(terms), 2)]
                m[at(i, l)] = value + terms[0]
        upper = [row_of(pivot[home], r) for r in range(SUB)]
        inv_tiles = [jnp.zeros(tile, F32) for _ in halves]
        fac_tiles = [jnp.zeros(tile, F32) for _ in halves]
        for r in range(SUB):
            for j in range(r):
                upper[r] = upper[r] - ratios[r, j] * upper[j]
                for l in halves:
                    rows[r][l] = rows[r][l] - ratios[r, j] * rows[j][l]
            here = subs == r
            for l in halves:
                if l <= home:
                    inv_tiles[l] = jnp.where(here, rows[r][l] * roots[r], inv_tiles[l])
                if l > home:
                    fac_tiles[l] = jnp.where(here, rows[r][l] * roots[r], fac_tiles[l])
                if l == home:
                    fac_tiles[l] = jnp.where(here, upper[r] * roots[r], fac_tiles[l])
        inv_tiles[home] = jnp.where(lanes < first + SUB, inv_tiles[home], 0.0)
        fac_tiles[home] = jnp.where(lanes - first >= subs, fac_tiles[home], 0.0)
        for l in halves:
            inv_v[at(g, l)] = inv_tiles[l] * SCALE
            factor[at(g, l)] = fac_tiles[l] * (1.0 / SCALE)

    turned = inv_v[...].T
    top = turned.astype(BF16)
    rest = (turned - top.astype(F32)).astype(BF16)
    load.wait()

    def store(i):
        return pltpu.make_async_copy(out_v.at[i], basis.at[i], sem.at[1 + i])

    @pl.loop(0, BLOCKS)
    def _(i):
        x = second_v[i]
        x_top = x.astype(BF16)
        x_rest = (x - x_top.astype(F32)).astype(BF16)
        out_v[i] = dot(x_top, top) + (dot(x_top, rest) + dot(x_rest, top))
        store(i).start()

    @pl.loop(0, BLOCKS)
    def _(i):
        store(i).wait()


def power_step(sketch, band_tiles, far_tiles, far_owner, far_local, far_count):
    any_space = pl.BlockSpec(memory_space=pl.ANY)
    scalars = pl.BlockSpec(memory_space=pltpu.SMEM)
    dma = pltpu.SemaphoreType.DMA
    return pl.pallas_call(
        range_kernel,
        out_shape=(
            jax.ShapeDtypeStruct((BLOCKS, B, B), F32),
            jax.ShapeDtypeStruct((B, B), F32),
        ),
        in_specs=[any_space, any_space, any_space, scalars, scalars, scalars],
        out_specs=(any_space, any_space),
        scratch_shapes=[
            pltpu.VMEM((UNITS, N_PANEL + 3, TALL, WIDE), BF16),
            pltpu.VMEM((UNITS, N_PANEL + 3, TALL, WIDE), BF16),
            pltpu.VMEM((BLOCKS, 3, B, B), BF16),
            pltpu.VMEM((BLOCKS, SLOTS, B, B), BF16),
            pltpu.VMEM((BLOCKS, B, B), F32),
            pltpu.VMEM((UNITS, 8, CAP, TALL, WIDE), BF16),
            pltpu.VMEM((B, B), F32),
            pltpu.VMEM((B, B), F32),
            pltpu.VMEM((N_ROW, PART, B), F32),
            pltpu.VMEM((N_GRP, PART, B), F32),
            pltpu.VMEM((8, 128), jnp.int32),
            pltpu.VMEM((4, 8, 128), jnp.int32),
            pltpu.VMEM((8, 128), jnp.int32),
            pltpu.SMEM((4, 8, 128), jnp.int32),
            pltpu.SMEM((8, 128), jnp.int32),
            dma((2 + UNITS,)),
            dma((2, UNITS, N_ROW)),
            dma((2, UNITS)),
            dma((2, 4)),
            dma((2, 4)),
            dma((4,)),
            dma((4,)),
            dma((2,)),
            dma((N_ROW,)),
            dma((N_ROW,)),
            dma((N_GRP,)),
            dma((N_GRP,)),
            dma((N_ROW,)),
            dma((N_ROW,)),
            dma((2,)),
        ],
        compiler_params=pltpu.CompilerParams(
            collective_id=0, has_side_effects=True, vmem_limit_bytes=58 * 1024 * 1024
        ),
        cost_estimate=pl.CostEstimate(
            flops=4 * 88 * B**3, bytes_accessed=15 << 20, transcendentals=0
        ),
    )(sketch, band_tiles, far_tiles, far_owner, far_local, far_count)


def orthonormalize(gram, second):
    whole = pl.BlockSpec(memory_space=pltpu.VMEM)
    any_space = pl.BlockSpec(memory_space=pl.ANY)
    return pl.pallas_call(
        factor_kernel,
        out_shape=(
            jax.ShapeDtypeStruct((BLOCKS, B, B), F32),
            jax.ShapeDtypeStruct((B, B), F32),
        ),
        in_specs=[whole, any_space],
        out_specs=(any_space, whole),
        scratch_shapes=[
            pltpu.VMEM((B, B), F32),
            pltpu.VMEM((B, B), F32),
            pltpu.VMEM((BLOCKS, B, B), F32),
            pltpu.VMEM((BLOCKS, B, B), F32),
            pltpu.SemaphoreType.DMA((1 + BLOCKS,)),
        ],
        compiler_params=pltpu.CompilerParams(vmem_limit_bytes=58 * 1024 * 1024),
    )(gram, second)


def body(sketch, band_tiles, far_tiles, far_owner, far_local, far_count):
    second, gram = power_step(sketch, band_tiles, far_tiles, far_owner, far_local, far_count)
    return orthonormalize(gram, second)


def solution(mesh):
    in_specs = (
        P(("row", "grp"), None, None),
        P(("row", "grp"), None, None, None),
        P(("row", "grp"), None, None, None),
        P(("row", "grp"), None),
        P(("row", "grp"), None),
        P(("row", "grp")),
    )
    out_specs = (P(("row", "grp"), None, None), P())
    return jax.shard_map(body, mesh=mesh, in_specs=in_specs, out_specs=out_specs, check_vma=False)
```

```python
import math

import jax
import jax.numpy as jnp
from jax import lax
from jax.experimental import pallas as pl
from jax.experimental.pallas import tpu as pltpu
from jax.sharding import PartitionSpec as P

MESH = pl.DeviceIdType.MESH
SIDE = 4
N_ROW = SIDE * SIDE
N_GRP = 8
BLOCKS = 8
SLOTS = 8
B = 256
N_PANEL = N_ROW * BLOCKS
ZERO, LEFT, RIGHT = N_PANEL, N_PANEL + 1, N_PANEL + 2
PART = B // N_ROW
CAP = 6
QUARTERS = 4
UNITS = 8
TALL, WIDE = B // 4, B // 2
F32 = jnp.float32
BF16 = jnp.bfloat16
SUB, LANE = 8, 128
SCALE = math.sqrt(BLOCKS * B * N_ROW * N_GRP)


def dot(a, b):
    return jnp.dot(a, b, preferred_element_type=F32)


def range_kernel(
    sketch, band, far, owner, local, count,
    second_out, gram_out,
    panel_a, panel_b, band_v, far_v, acc, packed, gram_v, gram_c, parts, shares, pair,
    wants_v, wants_in, index_v, wants_s, index_s,
    load_sem, recv_sem, send_sem, halo_send, halo_recv, wants_send, wants_recv, table_sem,
    scatter_send, scatter_recv, share_send, share_recv, spread_send, spread_recv, out_sem,
):
    row, grp = lax.axis_index("row"), lax.axis_index("grp")
    x, z = row // SIDE, row % SIDE
    device = row * N_GRP + grp
    after, before = (device + 1) % (N_ROW * N_GRP), (device + N_ROW * N_GRP - 1) % (N_ROW * N_GRP)
    after_id = (after // N_GRP, after % N_GRP)
    before_id = (before // N_GRP, before % N_GRP)
    own = row * BLOCKS
    y, core = grp // 2, grp % 2
    around = (
        ((x + 1) % SIDE * SIDE + z, 1),
        ((x + SIDE - 1) % SIDE * SIDE + z, 0),
        (x * SIDE + (z + 1) % SIDE, 3),
        (x * SIDE + (z + SIDE - 1) % SIDE, 2),
    )

    def along(k):
        return (y + k) % SIDE * 2 + core


    def load_unit(n):
        h, q = n // QUARTERS, n % QUARTERS
        return pltpu.make_async_copy(
            sketch.at[:, pl.ds(q * TALL, TALL), pl.ds(h * WIDE, WIDE)],
            panel_a.at[n, pl.ds(own, BLOCKS)],
            load_sem.at[2 + n],
        )

    load_band = pltpu.make_async_copy(band, band_v, load_sem.at[0])
    load_far = pltpu.make_async_copy(far, far_v, load_sem.at[1])
    for n in range(UNITS):
        load_unit(n).start()
    load_band.start()
    load_far.start()

    barrier = pltpu.get_barrier_semaphore()

    def greet(device_id):
        pl.semaphore_signal(barrier, inc=1, device_id=device_id, device_id_type=MESH)

    for neighbour, _ in around:
        greet((neighbour, grp))
    greet(after_id)
    greet(before_id)
    for k in range(1, SIDE):
        greet((row, along(k)))

    table = (8, 128)
    lanes = lax.broadcasted_iota(jnp.int32, table, 1)
    subs = lax.broadcasted_iota(jnp.int32, table, 0)
    nothing = jnp.zeros(table, jnp.int32)

    def spread_entry(e, carry):
        owners, locals_, counts = carry
        i, s = e // SLOTS, e % SLOTS
        here = lanes == e
        return (
            jnp.where(here, owner[i, s], owners),
            jnp.where(here, local[i, s], locals_),
            jnp.where(here, count[i], counts),
        )

    owners, locals_, counts = lax.fori_loop(
        0, BLOCKS * SLOTS, spread_entry, (nothing, nothing, nothing)
    )

    def rank_entry(e, carry):
        wants, seen, ranks = carry
        i, s = e // SLOTS, e % SLOTS
        name = owner[i, s]
        hit = (lanes // SLOTS) == name
        wants = jnp.where(hit & (seen == lanes % SLOTS), local[i, s], wants)
        seen = seen + hit.astype(jnp.int32)
        ranks = ranks + ((owners == name) & (lanes > e)).astype(jnp.int32)
        return wants, seen, ranks

    wants, _, ranks = lax.fori_loop(
        0, BLOCKS * SLOTS, rank_entry, (nothing, nothing, nothing)
    )
    wants_v[...] = wants
    from_x = (x - owners // SIDE + SIDE) % SIDE
    from_z = (z - owners % SIDE + SIDE) % SIDE
    index = nothing
    for q in range(QUARTERS):
        away = from_z if q % 2 == 0 else from_x
        if q // 2 == 1:
            away = (SIDE - away) % SIDE
        leaf = away // 2
        at = owners * BLOCKS + locals_ + leaf * (ranks - locals_)
        at = jnp.where(lanes % SLOTS < counts, at, ZERO)
        index = jnp.where(subs == q, at, index)
    index_v[...] = index
    index_copy = pltpu.make_async_copy(index_v, index_s, table_sem.at[0])
    index_copy.start()

    for panel in (panel_a, panel_b):
        panel[:, ZERO] = jnp.zeros((UNITS, TALL, WIDE), BF16)
    for n in range(UNITS):
        load_unit(n).wait()
    pl.semaphore_wait(barrier, len(around) + 2 + SIDE - 1)

    tell = [
        pltpu.make_async_remote_copy(
            src_ref=wants_v,
            dst_ref=wants_in.at[side],
            send_sem=wants_send.at[side],
            recv_sem=wants_recv.at[side],
            device_id=(neighbour, grp),
            device_id_type=MESH,
        )
        for neighbour, side in around
    ]
    for one in tell:
        one.start()

    def gather_steps(app, panel):
        def turn(n):
            return n % 2, 1 - 2 * ((n // 2) % 2)

        def place(n, first, second):
            swap, sign = turn(n)
            to_x = (x + 2 * SIDE + sign * (first * (1 - swap) + second * swap)) % SIDE
            to_z = (z + 2 * SIDE + sign * (first * swap + second * (1 - swap))) % SIDE
            return to_x * SIDE + to_z

        def send(n, u, v, first, second):
            slots = pl.ds(place(n, -u, -v) * BLOCKS, BLOCKS)
            to_u, to_v = (u + first) % SIDE, (v + second) % SIDE
            pltpu.make_async_remote_copy(
                src_ref=panel.at[n, slots],
                dst_ref=panel.at[n, slots],
                send_sem=send_sem.at[app, n],
                recv_sem=recv_sem.at[app, n, to_u * SIDE + to_v],
                device_id=(place(n, first, second), grp),
                device_id_type=MESH,
            ).start()

        def send_leaf(n, u, v, second):
            swap, sign = turn(n)
            side = 2 * (1 - swap) + (1 - second * sign) // 2
            source = place(n, -u, -v)
            to_v = (v + second) % SIDE
            leaf = u * 2 + to_v - 2
            blocks = [panel[n, source * BLOCKS + b] for b in range(BLOCKS)]
            for k in range(CAP):
                wanted = wants_s[side, 0, source * SLOTS + k]
                out = blocks[0]
                for b in range(1, BLOCKS):
                    out = jnp.where(wanted == b, blocks[b], out)
                packed[n, leaf, k] = out
            pltpu.make_async_remote_copy(
                src_ref=packed.at[n, leaf],
                dst_ref=panel.at[n, pl.ds(source * BLOCKS, CAP)],
                send_sem=send_sem.at[app, n],
                recv_sem=recv_sem.at[app, n, u * SIDE + to_v],
                device_id=(place(n, 0, second), grp),
                device_id_type=MESH,
            ).start()

        def arrived(n, u, v):
            slots = pl.ds(place(n, -u, -v) * BLOCKS, CAP if v >= 2 else BLOCKS)
            pltpu.make_async_copy(
                panel.at[n, slots], panel.at[n, slots], recv_sem.at[app, n, u * SIDE + v]
            ).wait()

        def send_own(n):
            send(n, 0, 0, 1, 0)
            send(n, 0, 0, -1, 0)
            send(n, 0, 0, 0, 1)

        def forward(meanwhile):
            @pl.loop(0, UNITS)
            def _(n):
                send_leaf(n, 0, 0, -1)

            meanwhile()

            @pl.loop(0, UNITS)
            def _(n):
                arrived(n, 1, 0)
                send(n, 1, 0, 1, 0)
                send(n, 1, 0, 0, 1)
                send_leaf(n, 1, 0, -1)
                arrived(n, 3, 0)
                send(n, 3, 0, 0, 1)
                send_leaf(n, 3, 0, -1)

            @pl.loop(0, UNITS)
            def _(n):
                arrived(n, 2, 0)
                send(n, 2, 0, 0, 1)
                send_leaf(n, 2, 0, -1)
                arrived(n, 0, 1)
                send_leaf(n, 0, 1, 1)

            @pl.loop(0, UNITS)
            def _(n):
                arrived(n, 1, 1)
                send_leaf(n, 1, 1, 1)
                arrived(n, 3, 1)
                send_leaf(n, 3, 1, 1)

            @pl.loop(0, UNITS)
            def _(n):
                arrived(n, 2, 1)
                send_leaf(n, 2, 1, 1)

            @pl.loop(0, UNITS)
            def _(n):
                for u in range(SIDE):
                    arrived(n, u, 3)
                for u in range(SIDE):
                    arrived(n, u, 2)

        def clear():
            @pl.loop(0, UNITS)
            def _(n):
                for u in range(SIDE):
                    for v in (2, 3):
                        for k in range(CAP, BLOCKS):
                            panel[n, place(n, -u, -v) * BLOCKS + k] = jnp.zeros((TALL, WIDE), BF16)

        def sent():
            total = 7 * BLOCKS + 8 * CAP

            @pl.loop(0, UNITS)
            def _(n):
                pltpu.make_async_copy(
                    panel.at[n, pl.ds(0, total)],
                    panel.at[n, pl.ds(0, total)],
                    send_sem.at[app, n],
                ).wait()

        return send_own, forward, sent, clear

    def halo(app, panel, h):
        units = pl.ds(h * QUARTERS, QUARTERS)
        tail = pltpu.make_async_remote_copy(
            src_ref=panel.at[units, own + BLOCKS - 1],
            dst_ref=panel.at[units, LEFT],
            send_sem=halo_send.at[app, 2 * h],
            recv_sem=halo_recv.at[app, 2 * h],
            device_id=after_id,
            device_id_type=MESH,
        )
        head = pltpu.make_async_remote_copy(
            src_ref=panel.at[units, own],
            dst_ref=panel.at[units, RIGHT],
            send_sem=halo_send.at[app, 2 * h + 1],
            recv_sem=halo_recv.at[app, 2 * h + 1],
            device_id=before_id,
            device_id_type=MESH,
        )
        return head, tail

    def column(panel, h, at):
        return jnp.concatenate(
            [panel[h * QUARTERS + q, at(q)] for q in range(QUARTERS)], axis=0
        )

    def block_of(panel, halves, at):
        return jnp.concatenate([column(panel, h, at) for h in halves], axis=1)

    def near(panel, i, halves):
        left = jnp.where(i == 0, jnp.where(device == 0, ZERO, LEFT), own + i - 1)
        right = jnp.where(
            i == BLOCKS - 1,
            jnp.where(device == N_ROW * N_GRP - 1, ZERO, RIGHT),
            own + i + 1,
        )
        return (
            dot(band_v[i, 0], block_of(panel, halves, lambda q: left))
            + dot(band_v[i, 1], block_of(panel, halves, lambda q: own + i))
            + dot(band_v[i, 2], block_of(panel, halves, lambda q: right))
        )

    def long_range(panel, i, halves, total):
        for s in range(SLOTS):
            remote = block_of(panel, halves, lambda q: index_s[q, i * SLOTS + s])
            total = total + dot(far_v[i, s], remote)
        return total

    both = (0, 1)
    send_own, forward, sent_a, clear = gather_steps(0, panel_a)
    pl.loop(0, UNITS)(send_own)
    edges = [copy for h in both for copy in halo(0, panel_a, h)]
    for copy in edges:
        copy.start()
    clear()
    for one in tell:
        one.wait()
    wants_copy = pltpu.make_async_copy(wants_in, wants_s, table_sem.at[1])
    wants_copy.start()
    wants_copy.wait()
    index_copy.wait()

    def band_part(panel, edges):
        for copy in edges:
            copy.wait()

        @pl.loop(0, BLOCKS)
        def _(i):
            acc[i] = near(panel, i, both)

    load_band.wait()
    forward(lambda: band_part(panel_a, edges))
    load_far.wait()

    send_own, forward, sent_b, clear = gather_steps(1, panel_b)
    edges = []
    for h in both:

        @pl.loop(0, BLOCKS)
        def _(i):
            total = long_range(panel_a, i, (h,), acc[i, :, pl.ds(h * WIDE, WIDE)])
            value = total.astype(BF16)
            for q in range(QUARTERS):
                panel_b[h * QUARTERS + q, own + i] = value[q * TALL : (q + 1) * TALL]

        pl.loop(h * QUARTERS, (h + 1) * QUARTERS)(send_own)
        edges += halo(1, panel_b, h)
        for copy in edges[-2:]:
            copy.start()

    sent_a()
    clear()
    forward(lambda: band_part(panel_b, edges))

    gram_v[...] = jnp.zeros((B, B), F32)
    gram_c[...] = jnp.zeros((B, B), F32)

    def add_gram(block):
        top = block.astype(BF16)
        rest = block - top.astype(F32)
        middle = rest.astype(BF16)
        low = (rest - middle.astype(F32)).astype(BF16)
        top_t = top.T
        gram_v[...] += dot(top_t, top) + dot(middle.T, middle)
        gram_c[...] += dot(top_t, middle) + dot(top_t, low)

    acc[0] = long_range(panel_b, 0, both, acc[0])

    @pl.loop(1, BLOCKS)
    def _(i):
        done = acc[i - 1]
        total = long_range(panel_b, i, both, acc[i])
        add_gram(done)
        acc[i] = total

    add_gram(acc[BLOCKS - 1])
    store = pltpu.make_async_copy(acc, second_out, out_sem.at[0])
    store.start()
    cross = gram_c[...]
    gram_v[...] += cross + cross.T

    def scatter(k):
        to = (row + k) % N_ROW
        return pltpu.make_async_remote_copy(
            src_ref=gram_v.at[pl.ds(to * PART, PART)],
            dst_ref=parts.at[row],
            send_sem=scatter_send.at[k],
            recv_sem=scatter_recv.at[k],
            device_id=(to, grp),
            device_id_type=MESH,
        )

    @pl.loop(1, N_ROW)
    def _(k):
        scatter(k).start()

    parts[row] = gram_v[pl.ds(row * PART, PART)]

    @pl.loop(1, N_ROW)
    def _(k):
        origin = (row + N_ROW - k) % N_ROW
        pltpu.make_async_copy(parts.at[origin], parts.at[origin], scatter_recv.at[k]).wait()

    total = parts[0]
    for k in range(1, N_ROW):
        total = total + parts[k]
    shares[y] = total

    def share(k):
        return pltpu.make_async_remote_copy(
            src_ref=shares.at[y],
            dst_ref=shares.at[y],
            send_sem=share_send.at[k],
            recv_sem=share_recv.at[k],
            device_id=(row, along(k)),
            device_id_type=MESH,
        )

    for k in range(1, SIDE):
        share(k).start()
    for k in range(1, SIDE):
        origin = (y + SIDE - k) % SIDE
        pltpu.make_async_copy(shares.at[origin], shares.at[origin], share_recv.at[k]).wait()
    pair[0] = (shares[0] + shares[1]) + (shares[2] + shares[3])
    swap = pltpu.make_async_remote_copy(
        src_ref=pair.at[0],
        dst_ref=pair.at[1],
        send_sem=share_send.at[0],
        recv_sem=share_recv.at[0],
        device_id=(row, y * 2 + 1 - core),
        device_id_type=MESH,
    )
    swap.start()
    swap.wait()
    total = pair[0] + pair[1]
    gram_c[pl.ds(row * PART, PART)] = total

    def spread(k):
        mine = pl.ds(row * PART, PART)
        return pltpu.make_async_remote_copy(
            src_ref=gram_c.at[mine],
            dst_ref=gram_c.at[mine],
            send_sem=spread_send.at[k],
            recv_sem=spread_recv.at[k],
            device_id=((row + k) % N_ROW, grp),
            device_id_type=MESH,
        )

    @pl.loop(1, N_ROW)
    def _(k):
        spread(k).start()

    @pl.loop(1, N_ROW)
    def _(k):
        theirs = pl.ds(((row + N_ROW - k) % N_ROW) * PART, PART)
        pltpu.make_async_copy(gram_c.at[theirs], gram_c.at[theirs], spread_recv.at[k]).wait()

    @pl.loop(1, N_ROW)
    def _(k):
        scatter(k).wait_send()
        spread(k).wait_send()

    for k in range(1, SIDE):
        share(k).wait_send()

    finish = pltpu.make_async_copy(gram_c, gram_out, out_sem.at[1])
    finish.start()
    sent_b()
    store.wait()
    finish.wait()


def factor_kernel(gram, second, basis, factor, m, inv_v, second_v, out_v, sem):
    load = pltpu.make_async_copy(second, second_v, sem.at[0])
    load.start()
    tile = (SUB, LANE)
    halves = range(B // LANE)
    lanes = lax.broadcasted_iota(jnp.int32, tile, 1)
    subs = lax.broadcasted_iota(jnp.int32, tile, 0)
    m[...] = gram[...]

    def row_of(a, r):
        return jnp.broadcast_to(a[r : r + 1, :], tile)

    def column_of(a, c):
        return jnp.broadcast_to(a[:, c : c + 1], tile)

    def at(i, l):
        return (pl.ds(i * SUB, SUB), pl.ds(l * LANE, LANE))

    for g in range(B // SUB):
        home, first = g * SUB // LANE, g * SUB % LANE
        inside = (lanes >= first) & (lanes < first + SUB)
        pivot = [m[at(g, l)] for l in halves]
        columns = [column_of(pivot[home], first + c) for c in range(SUB)]
        s = {(r, c): row_of(columns[c], r) for c in range(SUB) for r in range(c, SUB)}
        roots, ratios = [], {}
        for j in range(SUB):
            d = s[j, j]
            inverse = 1.0 / d
            roots.append(lax.rsqrt(d))
            old = {r: s[max(r, j), min(r, j)] for r in range(SUB) if r != j}
            new = {r: old[r] * inverse for r in old}
            for r in old:
                for c in old:
                    if c <= r:
                        s[r, c] = s[r, c] - old[r] * new[c]
            for r in old:
                s[max(r, j), min(r, j)] = new[r]
                if r > j:
                    ratios[r, j] = new[r]
            s[j, j] = -inverse
        unit = jnp.where(inside, (lanes - first == subs).astype(F32), pivot[home])
        source = [unit if l == home else pivot[l] for l in halves]
        rows = [[row_of(source[l], r) for l in halves] for r in range(SUB)]
        weights = []
        for c in range(SUB):
            per = []
            for l in halves:
                terms = [s[max(r, c), min(r, c)] * rows[r][l] for r in range(SUB)]
                while len(terms) > 1:
                    terms = [terms[k] + terms[k + 1] for k in range(0, len(terms), 2)]
                per.append(terms[0])
            weights.append(per)
        for i in range(g + 1, B // SUB):
            left = m[at(i, home)]
            columns = [column_of(left, first + c) for c in range(SUB)]
            for l in halves:
                value = jnp.where(inside, 0.0, left) if l == home else m[at(i, l)]
                terms = [columns[c] * weights[c][l] for c in range(SUB)]
                while len(terms) > 1:
                    terms = [terms[k] + terms[k + 1] for k in range(0, len(terms), 2)]
                m[at(i, l)] = value + terms[0]
        upper = [row_of(pivot[home], r) for r in range(SUB)]
        inv_tiles = [jnp.zeros(tile, F32) for _ in halves]
        fac_tiles = [jnp.zeros(tile, F32) for _ in halves]
        for r in range(SUB):
            for j in range(r):
                upper[r] = upper[r] - ratios[r, j] * upper[j]
                for l in halves:
                    rows[r][l] = rows[r][l] - ratios[r, j] * rows[j][l]
            here = subs == r
            for l in halves:
                if l <= home:
                    inv_tiles[l] = jnp.where(here, rows[r][l] * roots[r], inv_tiles[l])
                if l > home:
                    fac_tiles[l] = jnp.where(here, rows[r][l] * roots[r], fac_tiles[l])
                if l == home:
                    fac_tiles[l] = jnp.where(here, upper[r] * roots[r], fac_tiles[l])
        inv_tiles[home] = jnp.where(lanes < first + SUB, inv_tiles[home], 0.0)
        fac_tiles[home] = jnp.where(lanes - first >= subs, fac_tiles[home], 0.0)
        for l in halves:
            inv_v[at(g, l)] = inv_tiles[l] * SCALE
            factor[at(g, l)] = fac_tiles[l] * (1.0 / SCALE)

    turned = inv_v[...].T
    top = turned.astype(BF16)
    rest = (turned - top.astype(F32)).astype(BF16)
    load.wait()

    def store(i):
        return pltpu.make_async_copy(out_v.at[i], basis.at[i], sem.at[1 + i])

    @pl.loop(0, BLOCKS)
    def _(i):
        x = second_v[i]
        x_top = x.astype(BF16)
        x_rest = (x - x_top.astype(F32)).astype(BF16)
        out_v[i] = dot(x_top, top) + (dot(x_top, rest) + dot(x_rest, top))
        store(i).start()

    @pl.loop(0, BLOCKS)
    def _(i):
        store(i).wait()


def power_step(sketch, band_tiles, far_tiles, far_owner, far_local, far_count):
    any_space = pl.BlockSpec(memory_space=pl.ANY)
    scalars = pl.BlockSpec(memory_space=pltpu.SMEM)
    dma = pltpu.SemaphoreType.DMA
    return pl.pallas_call(
        range_kernel,
        out_shape=(
            jax.ShapeDtypeStruct((BLOCKS, B, B), F32),
            jax.ShapeDtypeStruct((B, B), F32),
        ),
        in_specs=[any_space, any_space, any_space, scalars, scalars, scalars],
        out_specs=(any_space, any_space),
        scratch_shapes=[
            pltpu.VMEM((UNITS, N_PANEL + 3, TALL, WIDE), BF16),
            pltpu.VMEM((UNITS, N_PANEL + 3, TALL, WIDE), BF16),
            pltpu.VMEM((BLOCKS, 3, B, B), BF16),
            pltpu.VMEM((BLOCKS, SLOTS, B, B), BF16),
            pltpu.VMEM((BLOCKS, B, B), F32),
            pltpu.VMEM((UNITS, 8, CAP, TALL, WIDE), BF16),
            pltpu.VMEM((B, B), F32),
            pltpu.VMEM((B, B), F32),
            pltpu.VMEM((N_ROW, PART, B), F32),
            pltpu.VMEM((SIDE, PART, B), F32),
            pltpu.VMEM((2, PART, B), F32),
            pltpu.VMEM((8, 128), jnp.int32),
            pltpu.VMEM((4, 8, 128), jnp.int32),
            pltpu.VMEM((8, 128), jnp.int32),
            pltpu.SMEM((4, 8, 128), jnp.int32),
            pltpu.SMEM((8, 128), jnp.int32),
            dma((2 + UNITS,)),
            dma((2, UNITS, N_ROW)),
            dma((2, UNITS)),
            dma((2, 4)),
            dma((2, 4)),
            dma((4,)),
            dma((4,)),
            dma((2,)),
            dma((N_ROW,)),
            dma((N_ROW,)),
            dma((SIDE,)),
            dma((SIDE,)),
            dma((N_ROW,)),
            dma((N_ROW,)),
            dma((2,)),
        ],
        compiler_params=pltpu.CompilerParams(
            collective_id=0, has_side_effects=True, vmem_limit_bytes=58 * 1024 * 1024
        ),
        cost_estimate=pl.CostEstimate(
            flops=4 * 88 * B**3, bytes_accessed=15 << 20, transcendentals=0
        ),
    )(sketch, band_tiles, far_tiles, far_owner, far_local, far_count)


def orthonormalize(gram, second):
    whole = pl.BlockSpec(memory_space=pltpu.VMEM)
    any_space = pl.BlockSpec(memory_space=pl.ANY)
    return pl.pallas_call(
        factor_kernel,
        out_shape=(
            jax.ShapeDtypeStruct((BLOCKS, B, B), F32),
            jax.ShapeDtypeStruct((B, B), F32),
        ),
        in_specs=[whole, any_space],
        out_specs=(any_space, whole),
        scratch_shapes=[
            pltpu.VMEM((B, B), F32),
            pltpu.VMEM((B, B), F32),
            pltpu.VMEM((BLOCKS, B, B), F32),
            pltpu.VMEM((BLOCKS, B, B), F32),
            pltpu.SemaphoreType.DMA((1 + BLOCKS,)),
        ],
        compiler_params=pltpu.CompilerParams(vmem_limit_bytes=58 * 1024 * 1024),
    )(gram, second)


def body(sketch, band_tiles, far_tiles, far_owner, far_local, far_count):
    second, gram = power_step(sketch, band_tiles, far_tiles, far_owner, far_local, far_count)
    return orthonormalize(gram, second)


def solution(mesh):
    in_specs = (
        P(("row", "grp"), None, None),
        P(("row", "grp"), None, None, None),
        P(("row", "grp"), None, None, None),
        P(("row", "grp"), None),
        P(("row", "grp"), None),
        P(("row", "grp")),
    )
    out_specs = (P(("row", "grp"), None, None), P())
    return jax.shard_map(body, mesh=mesh, in_specs=in_specs, out_specs=out_specs, check_vma=False)
```

```python
import math

import jax
import jax.numpy as jnp
from jax import lax
from jax.experimental import pallas as pl
from jax.experimental.pallas import tpu as pltpu
from jax.sharding import PartitionSpec as P

MESH = pl.DeviceIdType.MESH
SIDE = 4
N_ROW = SIDE * SIDE
N_GRP = 8
BLOCKS = 8
SLOTS = 8
B = 256
N_PANEL = N_ROW * BLOCKS
ZERO, LEFT, RIGHT = N_PANEL, N_PANEL + 1, N_PANEL + 2
PART = B // N_ROW
CAP = 6
QUARTERS = 4
UNITS = 8
TALL, WIDE = B // 4, B // 2
TREE = (
    (((0, 0), ((1, 0), (0, 1), (-1, 0), (0, -1))),),
    (((1, 0), ((1, 0), (0, 1), (0, -1))), ((0, 1), ((0, 1), (-1, 0)))),
    (((2, 0), ((0, -1), (0, 1))), ((0, 2), ((1, 0), (-1, 0)))),
    (((2, 3), ((0, -1), (1, 0))),),
)
INNER = [node for level in TREE for node, _ in level]
LEAVES = [(u, v) for u in range(SIDE) for v in range(SIDE) if (u, v) not in INNER]
F32 = jnp.float32
BF16 = jnp.bfloat16
SUB, LANE = 8, 128
SCALE = math.sqrt(BLOCKS * B * N_ROW * N_GRP)


def dot(a, b):
    return jnp.dot(a, b, preferred_element_type=F32)


def range_kernel(
    sketch, band, far, owner_in, local_in, count_in,
    second_out, gram_out,
    panel_a, panel_b, band_v, far_v, acc, packed, gram_v, gram_c, parts, shares, pair,
    wants_v, wants_in, index_v, wants_s, index_s, owner, local, count,
    load_sem, recv_sem, send_sem, halo_send, halo_recv, wants_send, wants_recv, table_sem,
    scatter_send, scatter_recv, share_send, share_recv, spread_send, spread_recv, out_sem,
):
    row, grp = lax.axis_index("row"), lax.axis_index("grp")
    x, z = row // SIDE, row % SIDE
    device = row * N_GRP + grp
    after, before = (device + 1) % (N_ROW * N_GRP), (device + N_ROW * N_GRP - 1) % (N_ROW * N_GRP)
    after_id = (after // N_GRP, after % N_GRP)
    before_id = (before // N_GRP, before % N_GRP)
    own = row * BLOCKS
    y, core = grp // 2, grp % 2
    around = (
        ((x + 1) % SIDE * SIDE + z, 1),
        ((x + SIDE - 1) % SIDE * SIDE + z, 0),
        (x * SIDE + (z + 1) % SIDE, 3),
        (x * SIDE + (z + SIDE - 1) % SIDE, 2),
    )

    def along(k):
        return (y + k) % SIDE * 2 + core


    def load_unit(n):
        h, q = n // QUARTERS, n % QUARTERS
        return pltpu.make_async_copy(
            sketch.at[:, pl.ds(q * TALL, TALL), pl.ds(h * WIDE, WIDE)],
            panel_a.at[n, pl.ds(own, BLOCKS)],
            load_sem.at[2 + n],
        )

    barrier = pltpu.get_barrier_semaphore()

    def greet(device_id):
        pl.semaphore_signal(barrier, inc=1, device_id=device_id, device_id_type=MESH)

    for neighbour, _ in around:
        greet((neighbour, grp))
    greet(after_id)
    greet(before_id)
    for k in range(1, SIDE):
        greet((row, along(k)))

    load_band = pltpu.make_async_copy(band, band_v, load_sem.at[0])
    load_far = pltpu.make_async_copy(far, far_v, load_sem.at[1])
    for n in range(UNITS):
        load_unit(n).start()
    load_scalars = [
        pltpu.make_async_copy(source, target, load_sem.at[2 + UNITS + k])
        for k, (source, target) in enumerate(
            ((owner_in, owner), (local_in, local), (count_in, count))
        )
    ]
    for one in load_scalars:
        one.start()
    load_band.start()
    load_far.start()

    for n in range(UNITS):
        load_unit(n).wait()
    pl.semaphore_wait(barrier, len(around) + 2 + SIDE - 1)

    def gather_steps(app, panel):
        def turn(n):
            return n % 2, 1 - 2 * ((n // 2) % 2)

        def place(n, first, second):
            swap, sign = turn(n)
            to_x = (x + 2 * SIDE + sign * (first * (1 - swap) + second * swap)) % SIDE
            to_z = (z + 2 * SIDE + sign * (first * swap + second * (1 - swap))) % SIDE
            return to_x * SIDE + to_z

        def send(n, u, v, first, second):
            slots = pl.ds(place(n, -u, -v) * BLOCKS, BLOCKS)
            to_u, to_v = (u + first) % SIDE, (v + second) % SIDE
            pltpu.make_async_remote_copy(
                src_ref=panel.at[n, slots],
                dst_ref=panel.at[n, slots],
                send_sem=send_sem.at[app, n],
                recv_sem=recv_sem.at[app, n, to_u * SIDE + to_v],
                device_id=(place(n, first, second), grp),
                device_id_type=MESH,
            ).start()

        def send_leaf(n, u, v, first, second):
            swap, sign = turn(n)
            side = 2 * (swap if first else 1 - swap) + (1 - (first + second) * sign) // 2
            source = place(n, -u, -v)
            to = ((u + first) % SIDE, (v + second) % SIDE)
            leaf = LEAVES.index(to)
            blocks = [panel[n, source * BLOCKS + b] for b in range(BLOCKS)]
            for k in range(CAP):
                wanted = wants_s[side, 0, source * SLOTS + k]
                out = blocks[0]
                for b in range(1, BLOCKS):
                    out = jnp.where(wanted == b, blocks[b], out)
                packed[n, leaf, k] = out
            pltpu.make_async_remote_copy(
                src_ref=packed.at[n, leaf],
                dst_ref=panel.at[n, pl.ds(source * BLOCKS, CAP)],
                send_sem=send_sem.at[app, n],
                recv_sem=recv_sem.at[app, n, to[0] * SIDE + to[1]],
                device_id=(place(n, first, second), grp),
                device_id_type=MESH,
            ).start()

        def arrived(n, u, v):
            slots = pl.ds(place(n, -u, -v) * BLOCKS, CAP if (u, v) in LEAVES else BLOCKS)
            pltpu.make_async_copy(
                panel.at[n, slots], panel.at[n, slots], recv_sem.at[app, n, u * SIDE + v]
            ).wait()

        def edges_of(n, node, steps, leaves):
            for first, second in steps:
                to = ((node[0] + first) % SIDE, (node[1] + second) % SIDE)
                if (to in LEAVES) == leaves:
                    (send_leaf if leaves else send)(n, *node, first, second)

        def send_own(n):
            edges_of(n, *TREE[0][0], False)

        def forward(meanwhile):
            @pl.loop(0, UNITS)
            def _(n):
                edges_of(n, *TREE[0][0], True)

            meanwhile()
            for level in TREE[1:]:

                @pl.loop(0, UNITS)
                def _(n):
                    for node, steps in level:
                        arrived(n, *node)
                        edges_of(n, node, steps, False)
                        edges_of(n, node, steps, True)

            @pl.loop(0, UNITS)
            def _(n):
                for node in LEAVES:
                    arrived(n, *node)

        def clear():
            @pl.loop(0, UNITS)
            def _(n):
                for u, v in LEAVES:
                    for k in range(CAP, BLOCKS):
                        panel[n, place(n, -u, -v) * BLOCKS + k] = jnp.zeros((TALL, WIDE), BF16)

        def sent():
            total = (len(INNER) - 1) * BLOCKS + len(LEAVES) * CAP

            @pl.loop(0, UNITS)
            def _(n):
                pltpu.make_async_copy(
                    panel.at[n, pl.ds(0, total)],
                    panel.at[n, pl.ds(0, total)],
                    send_sem.at[app, n],
                ).wait()

        return send_own, forward, sent, clear

    def halo(app, panel, h):
        units = pl.ds(h * QUARTERS, QUARTERS)
        tail = pltpu.make_async_remote_copy(
            src_ref=panel.at[units, own + BLOCKS - 1],
            dst_ref=panel.at[units, LEFT],
            send_sem=halo_send.at[app, 2 * h],
            recv_sem=halo_recv.at[app, 2 * h],
            device_id=after_id,
            device_id_type=MESH,
        )
        head = pltpu.make_async_remote_copy(
            src_ref=panel.at[units, own],
            dst_ref=panel.at[units, RIGHT],
            send_sem=halo_send.at[app, 2 * h + 1],
            recv_sem=halo_recv.at[app, 2 * h + 1],
            device_id=before_id,
            device_id_type=MESH,
        )
        return head, tail

    def column(panel, h, at):
        return jnp.concatenate(
            [panel[h * QUARTERS + q, at(q)] for q in range(QUARTERS)], axis=0
        )

    def block_of(panel, halves, at):
        return jnp.concatenate([column(panel, h, at) for h in halves], axis=1)

    def near(panel, i, halves):
        left = jnp.where(i == 0, jnp.where(device == 0, ZERO, LEFT), own + i - 1)
        right = jnp.where(
            i == BLOCKS - 1,
            jnp.where(device == N_ROW * N_GRP - 1, ZERO, RIGHT),
            own + i + 1,
        )
        return (
            dot(band_v[i, 0], block_of(panel, halves, lambda q: left))
            + dot(band_v[i, 1], block_of(panel, halves, lambda q: own + i))
            + dot(band_v[i, 2], block_of(panel, halves, lambda q: right))
        )

    def long_range(panel, i, halves, total):
        for s in range(SLOTS):
            remote = block_of(panel, halves, lambda q: index_s[q, i * SLOTS + s])
            total = total + dot(far_v[i, s], remote)
        return total

    both = (0, 1)
    send_own, forward, sent_a, clear = gather_steps(0, panel_a)
    pl.loop(0, UNITS)(send_own)
    edges = [copy for h in both for copy in halo(0, panel_a, h)]
    for copy in edges:
        copy.start()
    for one in load_scalars:
        one.wait()
    table = (8, 128)
    lanes = lax.broadcasted_iota(jnp.int32, table, 1)
    subs = lax.broadcasted_iota(jnp.int32, table, 0)
    nothing = jnp.zeros(table, jnp.int32)

    def spread_entry(e, carry):
        owners, locals_, counts = carry
        i, s = e // SLOTS, e % SLOTS
        here = lanes == e
        return (
            jnp.where(here, owner[i, s], owners),
            jnp.where(here, local[i, s], locals_),
            jnp.where(here, count[i], counts),
        )

    owners, locals_, counts = lax.fori_loop(
        0, BLOCKS * SLOTS, spread_entry, (nothing, nothing, nothing)
    )

    def rank_entry(e, carry):
        wants, seen, ranks = carry
        i, s = e // SLOTS, e % SLOTS
        name = owner[i, s]
        hit = (lanes // SLOTS) == name
        wants = jnp.where(hit & (seen == lanes % SLOTS), local[i, s], wants)
        seen = seen + hit.astype(jnp.int32)
        ranks = ranks + ((owners == name) & (lanes > e)).astype(jnp.int32)
        return wants, seen, ranks

    wants, _, ranks = lax.fori_loop(
        0, BLOCKS * SLOTS, rank_entry, (nothing, nothing, nothing)
    )
    wants_v[...] = wants
    from_x = (x - owners // SIDE + SIDE) % SIDE
    from_z = (z - owners % SIDE + SIDE) % SIDE
    index = nothing
    for q in range(QUARTERS):
        u, v = (from_x, from_z) if q % 2 == 0 else (from_z, from_x)
        if q // 2 == 1:
            u, v = (SIDE - u) % SIDE, (SIDE - v) % SIDE
        leaf = nothing
        for a, b in LEAVES:
            leaf = leaf + (u * SIDE + v == a * SIDE + b).astype(jnp.int32)
        at = owners * BLOCKS + locals_ + leaf * (ranks - locals_)
        at = jnp.where(lanes % SLOTS < counts, at, ZERO)
        index = jnp.where(subs == q, at, index)
    index_v[...] = index
    index_copy = pltpu.make_async_copy(index_v, index_s, table_sem.at[0])
    index_copy.start()

    tell = [
        pltpu.make_async_remote_copy(
            src_ref=wants_v,
            dst_ref=wants_in.at[side],
            send_sem=wants_send.at[side],
            recv_sem=wants_recv.at[side],
            device_id=(neighbour, grp),
            device_id_type=MESH,
        )
        for neighbour, side in around
    ]
    for one in tell:
        one.start()

    for panel in (panel_a, panel_b):
        panel[:, ZERO] = jnp.zeros((UNITS, TALL, WIDE), BF16)
    clear()
    for one in tell:
        one.wait()
    wants_copy = pltpu.make_async_copy(wants_in, wants_s, table_sem.at[1])
    wants_copy.start()
    wants_copy.wait()
    index_copy.wait()

    def band_part(panel, edges):
        for copy in edges:
            copy.wait()

        @pl.loop(0, BLOCKS)
        def _(i):
            acc[i] = near(panel, i, both)

    load_band.wait()
    forward(lambda: band_part(panel_a, edges))
    load_far.wait()

    send_own, forward, sent_b, clear = gather_steps(1, panel_b)
    edges = []
    for h in both:

        @pl.loop(0, BLOCKS)
        def _(i):
            total = long_range(panel_a, i, (h,), acc[i, :, pl.ds(h * WIDE, WIDE)])
            value = total.astype(BF16)
            for q in range(QUARTERS):
                panel_b[h * QUARTERS + q, own + i] = value[q * TALL : (q + 1) * TALL]

        pl.loop(h * QUARTERS, (h + 1) * QUARTERS)(send_own)
        edges += halo(1, panel_b, h)
        for copy in edges[-2:]:
            copy.start()

    sent_a()
    clear()
    forward(lambda: band_part(panel_b, edges))

    gram_v[...] = jnp.zeros((B, B), F32)
    gram_c[...] = jnp.zeros((B, B), F32)

    def add_gram(block):
        top = block.astype(BF16)
        rest = block - top.astype(F32)
        middle = rest.astype(BF16)
        low = (rest - middle.astype(F32)).astype(BF16)
        top_t = top.T
        gram_v[...] += dot(top_t, top) + dot(middle.T, middle)
        gram_c[...] += dot(top_t, middle) + dot(top_t, low)

    acc[0] = long_range(panel_b, 0, both, acc[0])

    @pl.loop(1, BLOCKS)
    def _(i):
        done = acc[i - 1]
        total = long_range(panel_b, i, both, acc[i])
        add_gram(done)
        acc[i] = total

    add_gram(acc[BLOCKS - 1])
    store = pltpu.make_async_copy(acc, second_out, out_sem.at[0])
    store.start()
    cross = gram_c[...]
    gram_v[...] += cross + cross.T

    def scatter(k):
        to = (row + k) % N_ROW
        return pltpu.make_async_remote_copy(
            src_ref=gram_v.at[pl.ds(to * PART, PART)],
            dst_ref=parts.at[row],
            send_sem=scatter_send.at[k],
            recv_sem=scatter_recv.at[k],
            device_id=(to, grp),
            device_id_type=MESH,
        )

    @pl.loop(1, N_ROW)
    def _(k):
        scatter(k).start()

    parts[row] = gram_v[pl.ds(row * PART, PART)]

    @pl.loop(1, N_ROW)
    def _(k):
        origin = (row + N_ROW - k) % N_ROW
        pltpu.make_async_copy(parts.at[origin], parts.at[origin], scatter_recv.at[k]).wait()

    total = parts[0]
    for k in range(1, N_ROW):
        total = total + parts[k]
    shares[y] = total

    def share(k):
        return pltpu.make_async_remote_copy(
            src_ref=shares.at[y],
            dst_ref=shares.at[y],
            send_sem=share_send.at[k],
            recv_sem=share_recv.at[k],
            device_id=(row, along(k)),
            device_id_type=MESH,
        )

    for k in range(1, SIDE):
        share(k).start()
    for k in range(1, SIDE):
        origin = (y + SIDE - k) % SIDE
        pltpu.make_async_copy(shares.at[origin], shares.at[origin], share_recv.at[k]).wait()
    pair[0] = (shares[0] + shares[1]) + (shares[2] + shares[3])
    swap = pltpu.make_async_remote_copy(
        src_ref=pair.at[0],
        dst_ref=pair.at[1],
        send_sem=share_send.at[0],
        recv_sem=share_recv.at[0],
        device_id=(row, y * 2 + 1 - core),
        device_id_type=MESH,
    )
    swap.start()
    swap.wait()
    total = pair[0] + pair[1]
    gram_c[pl.ds(row * PART, PART)] = total

    def spread(k):
        mine = pl.ds(row * PART, PART)
        return pltpu.make_async_remote_copy(
            src_ref=gram_c.at[mine],
            dst_ref=gram_c.at[mine],
            send_sem=spread_send.at[k],
            recv_sem=spread_recv.at[k],
            device_id=((row + k) % N_ROW, grp),
            device_id_type=MESH,
        )

    @pl.loop(1, N_ROW)
    def _(k):
        spread(k).start()

    @pl.loop(1, N_ROW)
    def _(k):
        theirs = pl.ds(((row + N_ROW - k) % N_ROW) * PART, PART)
        pltpu.make_async_copy(gram_c.at[theirs], gram_c.at[theirs], spread_recv.at[k]).wait()

    @pl.loop(1, N_ROW)
    def _(k):
        scatter(k).wait_send()
        spread(k).wait_send()

    for k in range(1, SIDE):
        share(k).wait_send()

    finish = pltpu.make_async_copy(gram_c, gram_out, out_sem.at[1])
    finish.start()
    sent_b()
    store.wait()
    finish.wait()


def factor_kernel(gram, second, basis, factor, m, inv_v, second_v, out_v, sem):
    load = pltpu.make_async_copy(second, second_v, sem.at[0])
    load.start()
    tile = (SUB, LANE)
    halves = range(B // LANE)
    lanes = lax.broadcasted_iota(jnp.int32, tile, 1)
    subs = lax.broadcasted_iota(jnp.int32, tile, 0)
    m[...] = gram[...]

    def row_of(a, r):
        return jnp.broadcast_to(a[r : r + 1, :], tile)

    def column_of(a, c):
        return jnp.broadcast_to(a[:, c : c + 1], tile)

    def at(i, l):
        return (pl.ds(i * SUB, SUB), pl.ds(l * LANE, LANE))

    for g in range(B // SUB):
        home, first = g * SUB // LANE, g * SUB % LANE
        inside = (lanes >= first) & (lanes < first + SUB)
        pivot = [m[at(g, l)] for l in halves]
        columns = [column_of(pivot[home], first + c) for c in range(SUB)]
        s = {(r, c): row_of(columns[c], r) for c in range(SUB) for r in range(c, SUB)}
        roots, ratios = [], {}
        for j in range(SUB):
            d = s[j, j]
            inverse = 1.0 / d
            roots.append(lax.rsqrt(d))
            old = {r: s[max(r, j), min(r, j)] for r in range(SUB) if r != j}
            new = {r: old[r] * inverse for r in old}
            for r in old:
                for c in old:
                    if c <= r:
                        s[r, c] = s[r, c] - old[r] * new[c]
            for r in old:
                s[max(r, j), min(r, j)] = new[r]
                if r > j:
                    ratios[r, j] = new[r]
            s[j, j] = -inverse
        unit = jnp.where(inside, (lanes - first == subs).astype(F32), pivot[home])
        source = [unit if l == home else pivot[l] for l in halves]
        rows = [[row_of(source[l], r) for l in halves] for r in range(SUB)]
        weights = []
        for c in range(SUB):
            per = []
            for l in halves:
                terms = [s[max(r, c), min(r, c)] * rows[r][l] for r in range(SUB)]
                while len(terms) > 1:
                    terms = [terms[k] + terms[k + 1] for k in range(0, len(terms), 2)]
                per.append(terms[0])
            weights.append(per)
        for i in range(g + 1, B // SUB):
            left = m[at(i, home)]
            columns = [column_of(left, first + c) for c in range(SUB)]
            for l in halves:
                value = jnp.where(inside, 0.0, left) if l == home else m[at(i, l)]
                terms = [columns[c] * weights[c][l] for c in range(SUB)]
                while len(terms) > 1:
                    terms = [terms[k] + terms[k + 1] for k in range(0, len(terms), 2)]
                m[at(i, l)] = value + terms[0]
        upper = [row_of(pivot[home], r) for r in range(SUB)]
        inv_tiles = [jnp.zeros(tile, F32) for _ in halves]
        fac_tiles = [jnp.zeros(tile, F32) for _ in halves]
        for r in range(SUB):
            for j in range(r):
                upper[r] = upper[r] - ratios[r, j] * upper[j]
                for l in halves:
                    rows[r][l] = rows[r][l] - ratios[r, j] * rows[j][l]
            here = subs == r
            for l in halves:
                if l <= home:
                    inv_tiles[l] = jnp.where(here, rows[r][l] * roots[r], inv_tiles[l])
                if l > home:
                    fac_tiles[l] = jnp.where(here, rows[r][l] * roots[r], fac_tiles[l])
                if l == home:
                    fac_tiles[l] = jnp.where(here, upper[r] * roots[r], fac_tiles[l])
        inv_tiles[home] = jnp.where(lanes < first + SUB, inv_tiles[home], 0.0)
        fac_tiles[home] = jnp.where(lanes - first >= subs, fac_tiles[home], 0.0)
        for l in halves:
            inv_v[at(g, l)] = inv_tiles[l] * SCALE
            factor[at(g, l)] = fac_tiles[l] * (1.0 / SCALE)

    turned = inv_v[...].T
    top = turned.astype(BF16)
    rest = (turned - top.astype(F32)).astype(BF16)
    load.wait()

    def store(i):
        return pltpu.make_async_copy(out_v.at[i], basis.at[i], sem.at[1 + i])

    @pl.loop(0, BLOCKS)
    def _(i):
        x = second_v[i]
        x_top = x.astype(BF16)
        x_rest = (x - x_top.astype(F32)).astype(BF16)
        out_v[i] = dot(x_top, top) + (dot(x_top, rest) + dot(x_rest, top))
        store(i).start()

    @pl.loop(0, BLOCKS)
    def _(i):
        store(i).wait()


def power_step(sketch, band_tiles, far_tiles, far_owner, far_local, far_count):
    any_space = pl.BlockSpec(memory_space=pl.ANY)
    dma = pltpu.SemaphoreType.DMA
    return pl.pallas_call(
        range_kernel,
        out_shape=(
            jax.ShapeDtypeStruct((BLOCKS, B, B), F32),
            jax.ShapeDtypeStruct((B, B), F32),
        ),
        in_specs=[any_space] * 6,
        out_specs=(any_space, any_space),
        scratch_shapes=[
            pltpu.VMEM((UNITS, N_PANEL + 3, TALL, WIDE), BF16),
            pltpu.VMEM((UNITS, N_PANEL + 3, TALL, WIDE), BF16),
            pltpu.VMEM((BLOCKS, 3, B, B), BF16),
            pltpu.VMEM((BLOCKS, SLOTS, B, B), BF16),
            pltpu.VMEM((BLOCKS, B, B), F32),
            pltpu.VMEM((UNITS, len(LEAVES), CAP, TALL, WIDE), BF16),
            pltpu.VMEM((B, B), F32),
            pltpu.VMEM((B, B), F32),
            pltpu.VMEM((N_ROW, PART, B), F32),
            pltpu.VMEM((SIDE, PART, B), F32),
            pltpu.VMEM((2, PART, B), F32),
            pltpu.VMEM((8, 128), jnp.int32),
            pltpu.VMEM((4, 8, 128), jnp.int32),
            pltpu.VMEM((8, 128), jnp.int32),
            pltpu.SMEM((4, 8, 128), jnp.int32),
            pltpu.SMEM((8, 128), jnp.int32),
            pltpu.SMEM((BLOCKS, SLOTS), jnp.int32),
            pltpu.SMEM((BLOCKS, SLOTS), jnp.int32),
            pltpu.SMEM((BLOCKS,), jnp.int32),
            dma((5 + UNITS,)),
            dma((2, UNITS, N_ROW)),
            dma((2, UNITS)),
            dma((2, 4)),
            dma((2, 4)),
            dma((4,)),
            dma((4,)),
            dma((2,)),
            dma((N_ROW,)),
            dma((N_ROW,)),
            dma((SIDE,)),
            dma((SIDE,)),
            dma((N_ROW,)),
            dma((N_ROW,)),
            dma((2,)),
        ],
        compiler_params=pltpu.CompilerParams(
            collective_id=0, has_side_effects=True, vmem_limit_bytes=58 * 1024 * 1024
        ),
        cost_estimate=pl.CostEstimate(
            flops=4 * 88 * B**3, bytes_accessed=15 << 20, transcendentals=0
        ),
    )(sketch, band_tiles, far_tiles, far_owner, far_local, far_count)


def orthonormalize(gram, second):
    whole = pl.BlockSpec(memory_space=pltpu.VMEM)
    any_space = pl.BlockSpec(memory_space=pl.ANY)
    return pl.pallas_call(
        factor_kernel,
        out_shape=(
            jax.ShapeDtypeStruct((BLOCKS, B, B), F32),
            jax.ShapeDtypeStruct((B, B), F32),
        ),
        in_specs=[whole, any_space],
        out_specs=(any_space, whole),
        scratch_shapes=[
            pltpu.VMEM((B, B), F32),
            pltpu.VMEM((B, B), F32),
            pltpu.VMEM((BLOCKS, B, B), F32),
            pltpu.VMEM((BLOCKS, B, B), F32),
            pltpu.SemaphoreType.DMA((1 + BLOCKS,)),
        ],
        compiler_params=pltpu.CompilerParams(vmem_limit_bytes=58 * 1024 * 1024),
    )(gram, second)


def body(sketch, band_tiles, far_tiles, far_owner, far_local, far_count):
    second, gram = power_step(sketch, band_tiles, far_tiles, far_owner, far_local, far_count)
    return orthonormalize(gram, second)


def solution(mesh):
    in_specs = (
        P(("row", "grp"), None, None),
        P(("row", "grp"), None, None, None),
        P(("row", "grp"), None, None, None),
        P(("row", "grp"), None),
        P(("row", "grp"), None),
        P(("row", "grp")),
    )
    out_specs = (P(("row", "grp"), None, None), P())
    return jax.shard_map(body, mesh=mesh, in_specs=in_specs, out_specs=out_specs, check_vma=False)
```

```python
import math

import jax
import jax.numpy as jnp
from jax import lax
from jax.experimental import pallas as pl
from jax.experimental.pallas import tpu as pltpu
from jax.sharding import PartitionSpec as P

MESH = pl.DeviceIdType.MESH
SIDE = 4
N_ROW = SIDE * SIDE
N_GRP = 8
BLOCKS = 8
SLOTS = 8
B = 256
N_PANEL = N_ROW * BLOCKS
ZERO, LEFT, RIGHT = N_PANEL, N_PANEL + 1, N_PANEL + 2
PART = B // N_ROW
CAP = 6
QUARTERS = 4
UNITS = 8
TALL, WIDE = B // 4, B // 2
TREE = (
    (((0, 0), ((1, 0), (0, 1), (-1, 0), (0, -1))),),
    (((1, 0), ((1, 0), (0, 1), (0, -1))), ((0, 1), ((0, 1), (-1, 0)))),
    (((2, 0), ((0, -1), (0, 1))), ((0, 2), ((1, 0), (-1, 0)))),
    (((2, 3), ((0, -1), (1, 0))),),
)
INNER = [node for level in TREE for node, _ in level]
LEAVES = [(u, v) for u in range(SIDE) for v in range(SIDE) if (u, v) not in INNER]
F32 = jnp.float32
BF16 = jnp.bfloat16
SUB, LANE = 8, 128
SCALE = math.sqrt(BLOCKS * B * N_ROW * N_GRP)


def dot(a, b):
    return jnp.dot(a, b, preferred_element_type=F32)


def range_kernel(
    sketch, band, far, owner_in, local_in, count_in,
    second_out, gram_out,
    panel_a0, panel_a1, panel_b0, panel_b1, band_v, far_v, acc, packed, gram_v, gram_c, parts, shares, pair,
    wants_v, wants_in, index_v, wants_s, index_s, owner, local, count,
    load_sem, recv_sem, send_sem, halo_send, halo_recv, wants_send, wants_recv, table_sem,
    scatter_send, scatter_recv, share_send, share_recv, spread_send, spread_recv, out_sem,
):
    row, grp = lax.axis_index("row"), lax.axis_index("grp")
    x, z = row // SIDE, row % SIDE
    device = row * N_GRP + grp
    after, before = (device + 1) % (N_ROW * N_GRP), (device + N_ROW * N_GRP - 1) % (N_ROW * N_GRP)
    after_id = (after // N_GRP, after % N_GRP)
    before_id = (before // N_GRP, before % N_GRP)
    own = row * BLOCKS
    panels_a, panels_b = (panel_a0, panel_a1), (panel_b0, panel_b1)
    y, core = grp // 2, grp % 2
    around = (
        ((x + 1) % SIDE * SIDE + z, 1),
        ((x + SIDE - 1) % SIDE * SIDE + z, 0),
        (x * SIDE + (z + 1) % SIDE, 3),
        (x * SIDE + (z + SIDE - 1) % SIDE, 2),
    )

    def along(k):
        return (y + k) % SIDE * 2 + core


    def load_unit(n):
        h, q = n // QUARTERS, n % QUARTERS
        return pltpu.make_async_copy(
            sketch.at[:, pl.ds(q * TALL, TALL), pl.ds(h * WIDE, WIDE)],
            panels_a[h].at[q, pl.ds(own, BLOCKS)],
            load_sem.at[2 + n],
        )

    barrier = pltpu.get_barrier_semaphore()

    def greet(device_id):
        pl.semaphore_signal(barrier, inc=1, device_id=device_id, device_id_type=MESH)

    for neighbour, _ in around:
        greet((neighbour, grp))
    greet(after_id)
    greet(before_id)
    for k in range(1, SIDE):
        greet((row, along(k)))

    load_band = pltpu.make_async_copy(band, band_v, load_sem.at[0])
    load_far = pltpu.make_async_copy(far, far_v, load_sem.at[1])
    for n in range(UNITS):
        load_unit(n).start()
    load_scalars = [
        pltpu.make_async_copy(source, target, load_sem.at[2 + UNITS + k])
        for k, (source, target) in enumerate(
            ((owner_in, owner), (local_in, local), (count_in, count))
        )
    ]
    for one in load_scalars:
        one.start()
    load_band.start()
    load_far.start()

    for n in range(UNITS):
        load_unit(n).wait()
    pl.semaphore_wait(barrier, len(around) + 2 + SIDE - 1)

    def gather_steps(app, h, panel):
        base = h * QUARTERS

        def turn(n):
            return n % 2, 1 - 2 * ((n // 2) % 2)

        def place(n, first, second):
            swap, sign = turn(n)
            to_x = (x + 2 * SIDE + sign * (first * (1 - swap) + second * swap)) % SIDE
            to_z = (z + 2 * SIDE + sign * (first * swap + second * (1 - swap))) % SIDE
            return to_x * SIDE + to_z

        def send(n, u, v, first, second):
            slots = pl.ds(place(n, -u, -v) * BLOCKS, BLOCKS)
            to_u, to_v = (u + first) % SIDE, (v + second) % SIDE
            pltpu.make_async_remote_copy(
                src_ref=panel.at[n, slots],
                dst_ref=panel.at[n, slots],
                send_sem=send_sem.at[app, base + n],
                recv_sem=recv_sem.at[app, base + n, to_u * SIDE + to_v],
                device_id=(place(n, first, second), grp),
                device_id_type=MESH,
            ).start()

        def send_leaf(n, u, v, first, second):
            swap, sign = turn(n)
            side = 2 * (swap if first else 1 - swap) + (1 - (first + second) * sign) // 2
            source = place(n, -u, -v)
            to = ((u + first) % SIDE, (v + second) % SIDE)
            leaf = LEAVES.index(to)
            blocks = [panel[n, source * BLOCKS + b] for b in range(BLOCKS)]
            for k in range(CAP):
                wanted = wants_s[side, 0, source * SLOTS + k]
                out = blocks[0]
                for b in range(1, BLOCKS):
                    out = jnp.where(wanted == b, blocks[b], out)
                packed[base + n, leaf, k] = out
            pltpu.make_async_remote_copy(
                src_ref=packed.at[base + n, leaf],
                dst_ref=panel.at[n, pl.ds(source * BLOCKS, CAP)],
                send_sem=send_sem.at[app, base + n],
                recv_sem=recv_sem.at[app, base + n, to[0] * SIDE + to[1]],
                device_id=(place(n, first, second), grp),
                device_id_type=MESH,
            ).start()

        def arrived(n, u, v):
            slots = pl.ds(place(n, -u, -v) * BLOCKS, CAP if (u, v) in LEAVES else BLOCKS)
            pltpu.make_async_copy(
                panel.at[n, slots], panel.at[n, slots], recv_sem.at[app, base + n, u * SIDE + v]
            ).wait()

        def edges_of(n, node, steps, leaves):
            for first, second in steps:
                to = ((node[0] + first) % SIDE, (node[1] + second) % SIDE)
                if (to in LEAVES) == leaves:
                    (send_leaf if leaves else send)(n, *node, first, second)

        def each(step):
            return lambda: pl.loop(0, QUARTERS)(step)

        def pass_on(depth):
            def step(n):
                for node, steps in TREE[depth]:
                    if depth:
                        arrived(n, *node)
                        edges_of(n, node, steps, False)
                    edges_of(n, node, steps, True)

            pl.loop(0, QUARTERS)(step)

        @each
        def send_own(n):
            edges_of(n, *TREE[0][0], False)

        @each
        def collect(n):
            for node in LEAVES:
                arrived(n, *node)

        @each
        def clear(n):
            for u, v in LEAVES:
                for k in range(CAP, BLOCKS):
                    panel[n, place(n, -u, -v) * BLOCKS + k] = jnp.zeros((TALL, WIDE), BF16)

        @each
        def sent(n):
            total = (len(INNER) - 1) * BLOCKS + len(LEAVES) * CAP
            pltpu.make_async_copy(
                panel.at[n, pl.ds(0, total)],
                panel.at[n, pl.ds(0, total)],
                send_sem.at[app, base + n],
            ).wait()

        return send_own, pass_on, collect, clear, sent

    def halo(app, panel, h):
        units = pl.ds(0, QUARTERS)
        tail = pltpu.make_async_remote_copy(
            src_ref=panel.at[units, own + BLOCKS - 1],
            dst_ref=panel.at[units, LEFT],
            send_sem=halo_send.at[app, 2 * h],
            recv_sem=halo_recv.at[app, 2 * h],
            device_id=after_id,
            device_id_type=MESH,
        )
        head = pltpu.make_async_remote_copy(
            src_ref=panel.at[units, own],
            dst_ref=panel.at[units, RIGHT],
            send_sem=halo_send.at[app, 2 * h + 1],
            recv_sem=halo_recv.at[app, 2 * h + 1],
            device_id=before_id,
            device_id_type=MESH,
        )
        return head, tail

    def column(panel, at):
        return jnp.concatenate([panel[q, at(q)] for q in range(QUARTERS)], axis=0)

    def block_of(panels, halves, at):
        return jnp.concatenate([column(panels[h], at) for h in halves], axis=1)

    def near(panel, i, halves):
        left = jnp.where(i == 0, jnp.where(device == 0, ZERO, LEFT), own + i - 1)
        right = jnp.where(
            i == BLOCKS - 1,
            jnp.where(device == N_ROW * N_GRP - 1, ZERO, RIGHT),
            own + i + 1,
        )
        return (
            dot(band_v[i, 0], block_of(panel, halves, lambda q: left))
            + dot(band_v[i, 1], block_of(panel, halves, lambda q: own + i))
            + dot(band_v[i, 2], block_of(panel, halves, lambda q: right))
        )

    def long_range(panel, i, halves, total):
        for s in range(SLOTS):
            remote = block_of(panel, halves, lambda q: index_s[q, i * SLOTS + s])
            total = total + dot(far_v[i, s], remote)
        return total

    both = (0, 1)
    gathers = [
        [gather_steps(app, h, panels[h]) for h in both]
        for app, panels in enumerate((panels_a, panels_b))
    ]
    (own_a0, pass_a0, collect_a0, clear_a0, sent_a0), (
        own_a1, pass_a1, collect_a1, clear_a1, sent_a1
    ) = gathers[0]
    (own_b0, pass_b0, collect_b0, clear_b0, sent_b0), (
        own_b1, pass_b1, collect_b1, clear_b1, sent_b1
    ) = gathers[1]

    own_a0()
    own_a1()
    edges_a = [copy for h in both for copy in halo(0, panels_a[h], h)]
    for copy in edges_a:
        copy.start()
    for one in load_scalars:
        one.wait()
    table = (8, 128)
    lanes = lax.broadcasted_iota(jnp.int32, table, 1)
    subs = lax.broadcasted_iota(jnp.int32, table, 0)
    nothing = jnp.zeros(table, jnp.int32)

    def spread_entry(e, carry):
        owners, locals_, counts = carry
        i, s = e // SLOTS, e % SLOTS
        here = lanes == e
        return (
            jnp.where(here, owner[i, s], owners),
            jnp.where(here, local[i, s], locals_),
            jnp.where(here, count[i], counts),
        )

    owners, locals_, counts = lax.fori_loop(
        0, BLOCKS * SLOTS, spread_entry, (nothing, nothing, nothing)
    )

    def rank_entry(e, carry):
        wants, seen, ranks = carry
        i, s = e // SLOTS, e % SLOTS
        name = owner[i, s]
        hit = (lanes // SLOTS) == name
        wants = jnp.where(hit & (seen == lanes % SLOTS), local[i, s], wants)
        seen = seen + hit.astype(jnp.int32)
        ranks = ranks + ((owners == name) & (lanes > e)).astype(jnp.int32)
        return wants, seen, ranks

    wants, _, ranks = lax.fori_loop(
        0, BLOCKS * SLOTS, rank_entry, (nothing, nothing, nothing)
    )
    wants_v[...] = wants
    from_x = (x - owners // SIDE + SIDE) % SIDE
    from_z = (z - owners % SIDE + SIDE) % SIDE
    index = nothing
    for q in range(QUARTERS):
        u, v = (from_x, from_z) if q % 2 == 0 else (from_z, from_x)
        if q // 2 == 1:
            u, v = (SIDE - u) % SIDE, (SIDE - v) % SIDE
        leaf = nothing
        for a, b in LEAVES:
            leaf = leaf + (u * SIDE + v == a * SIDE + b).astype(jnp.int32)
        at = owners * BLOCKS + locals_ + leaf * (ranks - locals_)
        at = jnp.where(lanes % SLOTS < counts, at, ZERO)
        index = jnp.where(subs == q, at, index)
    index_v[...] = index
    index_copy = pltpu.make_async_copy(index_v, index_s, table_sem.at[0])
    index_copy.start()

    tell = [
        pltpu.make_async_remote_copy(
            src_ref=wants_v,
            dst_ref=wants_in.at[side],
            send_sem=wants_send.at[side],
            recv_sem=wants_recv.at[side],
            device_id=(neighbour, grp),
            device_id_type=MESH,
        )
        for neighbour, side in around
    ]
    for one in tell:
        one.start()

    for panel in panels_a + panels_b:
        panel[:, ZERO] = jnp.zeros((QUARTERS, TALL, WIDE), BF16)
    clear_a0()
    clear_a1()
    clear_b0()
    clear_b1()
    for one in tell:
        one.wait()
    wants_copy = pltpu.make_async_copy(wants_in, wants_s, table_sem.at[1])
    wants_copy.start()
    wants_copy.wait()
    index_copy.wait()

    def band_part(panel, edges):
        for copy in edges:
            copy.wait()

        @pl.loop(0, BLOCKS)
        def _(i):
            acc[i] = near(panel, i, both)

    edges_b = []

    def first_half(h, send_half):
        @pl.loop(0, BLOCKS)
        def _(i):
            total = long_range(panels_a, i, (h,), acc[i, :, pl.ds(h * WIDE, WIDE)])
            value = total.astype(BF16)
            for q in range(QUARTERS):
                panels_b[h][q, own + i] = value[q * TALL : (q + 1) * TALL]

        send_half()
        copies = halo(1, panels_b[h], h)
        for copy in copies:
            copy.start()
        edges_b.extend(copies)

    pass_a0(0)
    pass_a1(0)
    load_band.wait()
    band_part(panels_a, edges_a)
    pass_a0(1)
    pass_a0(2)
    pass_a1(1)
    pass_a0(3)
    pass_a1(2)
    load_far.wait()
    collect_a0()
    first_half(0, own_b0)
    pass_a1(3)
    sent_a0()
    pass_b0(0)
    pass_b0(1)
    collect_a1()
    first_half(1, own_b1)
    sent_a1()
    pass_b1(0)
    band_part(panels_b, edges_b)
    pass_b0(2)
    pass_b1(1)
    pass_b0(3)
    pass_b1(2)
    pass_b1(3)
    collect_b0()
    collect_b1()

    gram_v[...] = jnp.zeros((B, B), F32)
    gram_c[...] = jnp.zeros((B, B), F32)

    def add_gram(block):
        top = block.astype(BF16)
        rest = block - top.astype(F32)
        middle = rest.astype(BF16)
        low = (rest - middle.astype(F32)).astype(BF16)
        top_t = top.T
        gram_v[...] += dot(top_t, top) + dot(middle.T, middle)
        gram_c[...] += dot(top_t, middle) + dot(top_t, low)

    acc[0] = long_range(panels_b, 0, both, acc[0])

    @pl.loop(1, BLOCKS)
    def _(i):
        done = acc[i - 1]
        total = long_range(panels_b, i, both, acc[i])
        add_gram(done)
        acc[i] = total

    add_gram(acc[BLOCKS - 1])
    store = pltpu.make_async_copy(acc, second_out, out_sem.at[0])
    store.start()
    cross = gram_c[...]
    gram_v[...] += cross + cross.T

    def scatter(k):
        to = (row + k) % N_ROW
        return pltpu.make_async_remote_copy(
            src_ref=gram_v.at[pl.ds(to * PART, PART)],
            dst_ref=parts.at[row],
            send_sem=scatter_send.at[k],
            recv_sem=scatter_recv.at[k],
            device_id=(to, grp),
            device_id_type=MESH,
        )

    @pl.loop(1, N_ROW)
    def _(k):
        scatter(k).start()

    parts[row] = gram_v[pl.ds(row * PART, PART)]

    @pl.loop(1, N_ROW)
    def _(k):
        origin = (row + N_ROW - k) % N_ROW
        pltpu.make_async_copy(parts.at[origin], parts.at[origin], scatter_recv.at[k]).wait()

    total = parts[0]
    for k in range(1, N_ROW):
        total = total + parts[k]
    shares[y] = total

    def share(k):
        return pltpu.make_async_remote_copy(
            src_ref=shares.at[y],
            dst_ref=shares.at[y],
            send_sem=share_send.at[k],
            recv_sem=share_recv.at[k],
            device_id=(row, along(k)),
            device_id_type=MESH,
        )

    for k in range(1, SIDE):
        share(k).start()
    for k in range(1, SIDE):
        origin = (y + SIDE - k) % SIDE
        pltpu.make_async_copy(shares.at[origin], shares.at[origin], share_recv.at[k]).wait()
    pair[0] = (shares[0] + shares[1]) + (shares[2] + shares[3])
    swap = pltpu.make_async_remote_copy(
        src_ref=pair.at[0],
        dst_ref=pair.at[1],
        send_sem=share_send.at[0],
        recv_sem=share_recv.at[0],
        device_id=(row, y * 2 + 1 - core),
        device_id_type=MESH,
    )
    swap.start()
    swap.wait()
    total = pair[0] + pair[1]
    gram_c[pl.ds(row * PART, PART)] = total

    def spread(k):
        mine = pl.ds(row * PART, PART)
        return pltpu.make_async_remote_copy(
            src_ref=gram_c.at[mine],
            dst_ref=gram_c.at[mine],
            send_sem=spread_send.at[k],
            recv_sem=spread_recv.at[k],
            device_id=((row + k) % N_ROW, grp),
            device_id_type=MESH,
        )

    @pl.loop(1, N_ROW)
    def _(k):
        spread(k).start()

    @pl.loop(1, N_ROW)
    def _(k):
        theirs = pl.ds(((row + N_ROW - k) % N_ROW) * PART, PART)
        pltpu.make_async_copy(gram_c.at[theirs], gram_c.at[theirs], spread_recv.at[k]).wait()

    finish = pltpu.make_async_copy(gram_c, gram_out, out_sem.at[1])
    finish.start()

    @pl.loop(1, N_ROW)
    def _(k):
        scatter(k).wait_send()
        spread(k).wait_send()

    for k in range(1, SIDE):
        share(k).wait_send()

    sent_b0()
    sent_b1()
    store.wait()
    finish.wait()


def factor_kernel(gram, second, basis, factor, m, inv_v, second_v, out_v, sem):
    load = pltpu.make_async_copy(second, second_v, sem.at[0])
    load.start()
    tile = (SUB, LANE)
    halves = range(B // LANE)
    lanes = lax.broadcasted_iota(jnp.int32, tile, 1)
    subs = lax.broadcasted_iota(jnp.int32, tile, 0)
    m[...] = gram[...]

    def row_of(a, r):
        return jnp.broadcast_to(a[r : r + 1, :], tile)

    def column_of(a, c):
        return jnp.broadcast_to(a[:, c : c + 1], tile)

    def at(i, l):
        return (pl.ds(i * SUB, SUB), pl.ds(l * LANE, LANE))

    for g in range(B // SUB):
        home, first = g * SUB // LANE, g * SUB % LANE
        inside = (lanes >= first) & (lanes < first + SUB)
        pivot = [m[at(g, l)] for l in halves]
        columns = [column_of(pivot[home], first + c) for c in range(SUB)]
        s = {(r, c): row_of(columns[c], r) for c in range(SUB) for r in range(c, SUB)}
        roots, ratios = [], {}
        for j in range(SUB):
            d = s[j, j]
            inverse = 1.0 / d
            roots.append(lax.rsqrt(d))
            old = {r: s[max(r, j), min(r, j)] for r in range(SUB) if r != j}
            new = {r: old[r] * inverse for r in old}
            for r in old:
                for c in old:
                    if c <= r:
                        s[r, c] = s[r, c] - old[r] * new[c]
            for r in old:
                s[max(r, j), min(r, j)] = new[r]
                if r > j:
                    ratios[r, j] = new[r]
            s[j, j] = -inverse
        unit = jnp.where(inside, (lanes - first == subs).astype(F32), pivot[home])
        source = [unit if l == home else pivot[l] for l in halves]
        rows = [[row_of(source[l], r) for l in halves] for r in range(SUB)]
        weights = []
        for c in range(SUB):
            per = []
            for l in halves:
                terms = [s[max(r, c), min(r, c)] * rows[r][l] for r in range(SUB)]
                while len(terms) > 1:
                    terms = [terms[k] + terms[k + 1] for k in range(0, len(terms), 2)]
                per.append(terms[0])
            weights.append(per)
        for i in range(g + 1, B // SUB):
            left = m[at(i, home)]
            columns = [column_of(left, first + c) for c in range(SUB)]
            for l in halves:
                value = jnp.where(inside, 0.0, left) if l == home else m[at(i, l)]
                terms = [columns[c] * weights[c][l] for c in range(SUB)]
                while len(terms) > 1:
                    terms = [terms[k] + terms[k + 1] for k in range(0, len(terms), 2)]
                m[at(i, l)] = value + terms[0]
        upper = [row_of(pivot[home], r) for r in range(SUB)]
        inv_tiles = [jnp.zeros(tile, F32) for _ in halves]
        fac_tiles = [jnp.zeros(tile, F32) for _ in halves]
        for r in range(SUB):
            for j in range(r):
                upper[r] = upper[r] - ratios[r, j] * upper[j]
                for l in halves:
                    rows[r][l] = rows[r][l] - ratios[r, j] * rows[j][l]
            here = subs == r
            for l in halves:
                if l <= home:
                    inv_tiles[l] = jnp.where(here, rows[r][l] * roots[r], inv_tiles[l])
                if l > home:
                    fac_tiles[l] = jnp.where(here, rows[r][l] * roots[r], fac_tiles[l])
                if l == home:
                    fac_tiles[l] = jnp.where(here, upper[r] * roots[r], fac_tiles[l])
        inv_tiles[home] = jnp.where(lanes < first + SUB, inv_tiles[home], 0.0)
        fac_tiles[home] = jnp.where(lanes - first >= subs, fac_tiles[home], 0.0)
        for l in halves:
            inv_v[at(g, l)] = inv_tiles[l] * SCALE
            factor[at(g, l)] = fac_tiles[l] * (1.0 / SCALE)

    turned = inv_v[...].T
    top = turned.astype(BF16)
    rest = (turned - top.astype(F32)).astype(BF16)
    load.wait()

    def store(i):
        return pltpu.make_async_copy(out_v.at[i], basis.at[i], sem.at[1 + i])

    @pl.loop(0, BLOCKS)
    def _(i):
        x = second_v[i]
        x_top = x.astype(BF16)
        x_rest = (x - x_top.astype(F32)).astype(BF16)
        out_v[i] = dot(x_top, top) + (dot(x_top, rest) + dot(x_rest, top))
        store(i).start()

    @pl.loop(0, BLOCKS)
    def _(i):
        store(i).wait()


def power_step(sketch, band_tiles, far_tiles, far_owner, far_local, far_count):
    any_space = pl.BlockSpec(memory_space=pl.ANY)
    dma = pltpu.SemaphoreType.DMA
    return pl.pallas_call(
        range_kernel,
        out_shape=(
            jax.ShapeDtypeStruct((BLOCKS, B, B), F32),
            jax.ShapeDtypeStruct((B, B), F32),
        ),
        in_specs=[any_space] * 6,
        out_specs=(any_space, any_space),
        scratch_shapes=[
            pltpu.VMEM((QUARTERS, N_PANEL + 3, TALL, WIDE), BF16),
            pltpu.VMEM((QUARTERS, N_PANEL + 3, TALL, WIDE), BF16),
            pltpu.VMEM((QUARTERS, N_PANEL + 3, TALL, WIDE), BF16),
            pltpu.VMEM((QUARTERS, N_PANEL + 3, TALL, WIDE), BF16),
            pltpu.VMEM((BLOCKS, 3, B, B), BF16),
            pltpu.VMEM((BLOCKS, SLOTS, B, B), BF16),
            pltpu.VMEM((BLOCKS, B, B), F32),
            pltpu.VMEM((UNITS, len(LEAVES), CAP, TALL, WIDE), BF16),
            pltpu.VMEM((B, B), F32),
            pltpu.VMEM((B, B), F32),
            pltpu.VMEM((N_ROW, PART, B), F32),
            pltpu.VMEM((SIDE, PART, B), F32),
            pltpu.VMEM((2, PART, B), F32),
            pltpu.VMEM((8, 128), jnp.int32),
            pltpu.VMEM((4, 8, 128), jnp.int32),
            pltpu.VMEM((8, 128), jnp.int32),
            pltpu.SMEM((4, 8, 128), jnp.int32),
            pltpu.SMEM((8, 128), jnp.int32),
            pltpu.SMEM((BLOCKS, SLOTS), jnp.int32),
            pltpu.SMEM((BLOCKS, SLOTS), jnp.int32),
            pltpu.SMEM((BLOCKS,), jnp.int32),
            dma((5 + UNITS,)),
            dma((2, UNITS, N_ROW)),
            dma((2, UNITS)),
            dma((2, 4)),
            dma((2, 4)),
            dma((4,)),
            dma((4,)),
            dma((2,)),
            dma((N_ROW,)),
            dma((N_ROW,)),
            dma((SIDE,)),
            dma((SIDE,)),
            dma((N_ROW,)),
            dma((N_ROW,)),
            dma((2,)),
        ],
        compiler_params=pltpu.CompilerParams(
            collective_id=0, has_side_effects=True, vmem_limit_bytes=58 * 1024 * 1024
        ),
        cost_estimate=pl.CostEstimate(
            flops=4 * 88 * B**3, bytes_accessed=15 << 20, transcendentals=0
        ),
    )(sketch, band_tiles, far_tiles, far_owner, far_local, far_count)


def orthonormalize(gram, second):
    whole = pl.BlockSpec(memory_space=pltpu.VMEM)
    any_space = pl.BlockSpec(memory_space=pl.ANY)
    return pl.pallas_call(
        factor_kernel,
        out_shape=(
            jax.ShapeDtypeStruct((BLOCKS, B, B), F32),
            jax.ShapeDtypeStruct((B, B), F32),
        ),
        in_specs=[whole, any_space],
        out_specs=(any_space, whole),
        scratch_shapes=[
            pltpu.VMEM((B, B), F32),
            pltpu.VMEM((B, B), F32),
            pltpu.VMEM((BLOCKS, B, B), F32),
            pltpu.VMEM((BLOCKS, B, B), F32),
            pltpu.SemaphoreType.DMA((1 + BLOCKS,)),
        ],
        compiler_params=pltpu.CompilerParams(vmem_limit_bytes=58 * 1024 * 1024),
    )(gram, second)


def body(sketch, band_tiles, far_tiles, far_owner, far_local, far_count):
    second, gram = power_step(sketch, band_tiles, far_tiles, far_owner, far_local, far_count)
    return orthonormalize(gram, second)


def solution(mesh):
    in_specs = (
        P(("row", "grp"), None, None),
        P(("row", "grp"), None, None, None),
        P(("row", "grp"), None, None, None),
        P(("row", "grp"), None),
        P(("row", "grp"), None),
        P(("row", "grp")),
    )
    out_specs = (P(("row", "grp"), None, None), P())
    return jax.shard_map(body, mesh=mesh, in_specs=in_specs, out_specs=out_specs, check_vma=False)
```

```python
import math

import jax
import jax.numpy as jnp
from jax import lax
from jax.experimental import pallas as pl
from jax.experimental.pallas import tpu as pltpu
from jax.sharding import PartitionSpec as P

MESH = pl.DeviceIdType.MESH
SIDE = 4
N_ROW = SIDE * SIDE
N_GRP = 8
BLOCKS = 8
SLOTS = 8
B = 256
N_PANEL = N_ROW * BLOCKS
ZERO, LEFT, RIGHT = N_PANEL, N_PANEL + 1, N_PANEL + 2
TRI = 3 * B // 2
PART = TRI // N_ROW
CAP = 6
QUARTERS = 4
UNITS = 8
TALL, WIDE = B // 4, B // 2
TREE = (
    (((0, 0), ((1, 0), (0, 1), (-1, 0), (0, -1))),),
    (((1, 0), ((1, 0), (0, 1), (0, -1))), ((0, 1), ((0, 1), (-1, 0)))),
    (((2, 0), ((0, -1), (0, 1))), ((0, 2), ((1, 0), (-1, 0)))),
    (((2, 3), ((0, -1), (1, 0))),),
)
INNER = [node for level in TREE for node, _ in level]
LEAVES = [(u, v) for u in range(SIDE) for v in range(SIDE) if (u, v) not in INNER]
F32 = jnp.float32
BF16 = jnp.bfloat16
SUB, LANE = 8, 128
SCALE = math.sqrt(BLOCKS * B * N_ROW * N_GRP)


def dot(a, b):
    return jnp.dot(a, b, preferred_element_type=F32)


def range_kernel(
    sketch, band, far, owner_in, local_in, count_in,
    second_out, gram_out,
    panel_a0, panel_a1, panel_b0, panel_b1, band_v, far_v, acc, packed, gram_v, gram_c, corner, summed, parts, shares, pair,
    wants_v, wants_in, index_v, wants_s, index_s, owner, local, count,
    load_sem, recv_sem, send_sem, halo_send, halo_recv, wants_send, wants_recv, table_sem,
    scatter_send, scatter_recv, share_send, share_recv, spread_send, spread_recv, out_sem,
):
    row, grp = lax.axis_index("row"), lax.axis_index("grp")
    x, z = row // SIDE, row % SIDE
    device = row * N_GRP + grp
    after, before = (device + 1) % (N_ROW * N_GRP), (device + N_ROW * N_GRP - 1) % (N_ROW * N_GRP)
    after_id = (after // N_GRP, after % N_GRP)
    before_id = (before // N_GRP, before % N_GRP)
    own = row * BLOCKS
    panels_a, panels_b = (panel_a0, panel_a1), (panel_b0, panel_b1)
    y, core = grp // 2, grp % 2
    around = (
        ((x + 1) % SIDE * SIDE + z, 1),
        ((x + SIDE - 1) % SIDE * SIDE + z, 0),
        (x * SIDE + (z + 1) % SIDE, 3),
        (x * SIDE + (z + SIDE - 1) % SIDE, 2),
    )

    def along(k):
        return (y + k) % SIDE * 2 + core


    def load_unit(n):
        h, q = n // QUARTERS, n % QUARTERS
        return pltpu.make_async_copy(
            sketch.at[:, pl.ds(q * TALL, TALL), pl.ds(h * WIDE, WIDE)],
            panels_a[h].at[q, pl.ds(own, BLOCKS)],
            load_sem.at[2 + n],
        )

    barrier = pltpu.get_barrier_semaphore()

    def greet(device_id):
        pl.semaphore_signal(barrier, inc=1, device_id=device_id, device_id_type=MESH)

    for neighbour, _ in around:
        greet((neighbour, grp))
    greet(after_id)
    greet(before_id)
    for k in range(1, SIDE):
        greet((row, along(k)))

    load_band = pltpu.make_async_copy(band, band_v, load_sem.at[0])
    load_far = pltpu.make_async_copy(far, far_v, load_sem.at[1])
    for n in range(UNITS):
        load_unit(n).start()
    load_scalars = [
        pltpu.make_async_copy(source, target, load_sem.at[2 + UNITS + k])
        for k, (source, target) in enumerate(
            ((owner_in, owner), (local_in, local), (count_in, count))
        )
    ]
    for one in load_scalars:
        one.start()
    load_band.start()
    load_far.start()

    for n in range(UNITS):
        load_unit(n).wait()
    pl.semaphore_wait(barrier, len(around) + 2 + SIDE - 1)

    def gather_steps(app, h, panel):
        base = h * QUARTERS

        def turn(n):
            return n % 2, 1 - 2 * ((n // 2) % 2)

        def place(n, first, second):
            swap, sign = turn(n)
            to_x = (x + 2 * SIDE + sign * (first * (1 - swap) + second * swap)) % SIDE
            to_z = (z + 2 * SIDE + sign * (first * swap + second * (1 - swap))) % SIDE
            return to_x * SIDE + to_z

        def send(n, u, v, first, second):
            slots = pl.ds(place(n, -u, -v) * BLOCKS, BLOCKS)
            to_u, to_v = (u + first) % SIDE, (v + second) % SIDE
            pltpu.make_async_remote_copy(
                src_ref=panel.at[n, slots],
                dst_ref=panel.at[n, slots],
                send_sem=send_sem.at[app, base + n],
                recv_sem=recv_sem.at[app, base + n, to_u * SIDE + to_v],
                device_id=(place(n, first, second), grp),
                device_id_type=MESH,
            ).start()

        def send_leaf(n, u, v, first, second):
            swap, sign = turn(n)
            side = 2 * (swap if first else 1 - swap) + (1 - (first + second) * sign) // 2
            source = place(n, -u, -v)
            to = ((u + first) % SIDE, (v + second) % SIDE)
            leaf = LEAVES.index(to)
            blocks = [panel[n, source * BLOCKS + b] for b in range(BLOCKS)]
            for k in range(CAP):
                wanted = wants_s[side, 0, source * SLOTS + k]
                out = blocks[0]
                for b in range(1, BLOCKS):
                    out = jnp.where(wanted == b, blocks[b], out)
                packed[base + n, leaf, k] = out
            pltpu.make_async_remote_copy(
                src_ref=packed.at[base + n, leaf],
                dst_ref=panel.at[n, pl.ds(source * BLOCKS, CAP)],
                send_sem=send_sem.at[app, base + n],
                recv_sem=recv_sem.at[app, base + n, to[0] * SIDE + to[1]],
                device_id=(place(n, first, second), grp),
                device_id_type=MESH,
            ).start()

        def arrived(n, u, v):
            slots = pl.ds(place(n, -u, -v) * BLOCKS, CAP if (u, v) in LEAVES else BLOCKS)
            pltpu.make_async_copy(
                panel.at[n, slots], panel.at[n, slots], recv_sem.at[app, base + n, u * SIDE + v]
            ).wait()

        def edges_of(n, node, steps, leaves):
            for first, second in steps:
                to = ((node[0] + first) % SIDE, (node[1] + second) % SIDE)
                if (to in LEAVES) == leaves:
                    (send_leaf if leaves else send)(n, *node, first, second)

        def each(step):
            return lambda: pl.loop(0, QUARTERS)(step)

        def pass_on(depth):
            def step(n):
                for node, steps in TREE[depth]:
                    if depth:
                        arrived(n, *node)
                        edges_of(n, node, steps, False)
                    edges_of(n, node, steps, True)

            pl.loop(0, QUARTERS)(step)

        @each
        def send_own(n):
            edges_of(n, *TREE[0][0], False)

        @each
        def collect(n):
            for node in LEAVES:
                arrived(n, *node)

        @each
        def clear(n):
            for u, v in LEAVES:
                for k in range(CAP, BLOCKS):
                    panel[n, place(n, -u, -v) * BLOCKS + k] = jnp.zeros((TALL, WIDE), BF16)

        @each
        def sent(n):
            total = (len(INNER) - 1) * BLOCKS + len(LEAVES) * CAP
            pltpu.make_async_copy(
                panel.at[n, pl.ds(0, total)],
                panel.at[n, pl.ds(0, total)],
                send_sem.at[app, base + n],
            ).wait()

        return send_own, pass_on, collect, clear, sent

    def halo(app, panel, h):
        units = pl.ds(0, QUARTERS)
        tail = pltpu.make_async_remote_copy(
            src_ref=panel.at[units, own + BLOCKS - 1],
            dst_ref=panel.at[units, LEFT],
            send_sem=halo_send.at[app, 2 * h],
            recv_sem=halo_recv.at[app, 2 * h],
            device_id=after_id,
            device_id_type=MESH,
        )
        head = pltpu.make_async_remote_copy(
            src_ref=panel.at[units, own],
            dst_ref=panel.at[units, RIGHT],
            send_sem=halo_send.at[app, 2 * h + 1],
            recv_sem=halo_recv.at[app, 2 * h + 1],
            device_id=before_id,
            device_id_type=MESH,
        )
        return head, tail

    def column(panel, at):
        return jnp.concatenate([panel[q, at(q)] for q in range(QUARTERS)], axis=0)

    def block_of(panels, halves, at):
        return jnp.concatenate([column(panels[h], at) for h in halves], axis=1)

    def near(panel, i, halves):
        left = jnp.where(i == 0, jnp.where(device == 0, ZERO, LEFT), own + i - 1)
        right = jnp.where(
            i == BLOCKS - 1,
            jnp.where(device == N_ROW * N_GRP - 1, ZERO, RIGHT),
            own + i + 1,
        )
        return (
            dot(band_v[i, 0], block_of(panel, halves, lambda q: left))
            + dot(band_v[i, 1], block_of(panel, halves, lambda q: own + i))
            + dot(band_v[i, 2], block_of(panel, halves, lambda q: right))
        )

    def long_range(panel, i, halves, total):
        for s in range(SLOTS):
            remote = block_of(panel, halves, lambda q: index_s[q, i * SLOTS + s])
            total = total + dot(far_v[i, s], remote)
        return total

    both = (0, 1)
    gathers = [
        [gather_steps(app, h, panels[h]) for h in both]
        for app, panels in enumerate((panels_a, panels_b))
    ]
    (own_a0, pass_a0, collect_a0, clear_a0, sent_a0), (
        own_a1, pass_a1, collect_a1, clear_a1, sent_a1
    ) = gathers[0]
    (own_b0, pass_b0, collect_b0, clear_b0, sent_b0), (
        own_b1, pass_b1, collect_b1, clear_b1, sent_b1
    ) = gathers[1]

    own_a0()
    own_a1()
    edges_a = [copy for h in both for copy in halo(0, panels_a[h], h)]
    for copy in edges_a:
        copy.start()
    for one in load_scalars:
        one.wait()
    table = (8, 128)
    lanes = lax.broadcasted_iota(jnp.int32, table, 1)
    subs = lax.broadcasted_iota(jnp.int32, table, 0)
    nothing = jnp.zeros(table, jnp.int32)

    def spread_entry(e, carry):
        owners, locals_, counts = carry
        i, s = e // SLOTS, e % SLOTS
        here = lanes == e
        return (
            jnp.where(here, owner[i, s], owners),
            jnp.where(here, local[i, s], locals_),
            jnp.where(here, count[i], counts),
        )

    owners, locals_, counts = lax.fori_loop(
        0, BLOCKS * SLOTS, spread_entry, (nothing, nothing, nothing)
    )

    def rank_entry(e, carry):
        wants, seen, ranks = carry
        i, s = e // SLOTS, e % SLOTS
        name = owner[i, s]
        hit = (lanes // SLOTS) == name
        wants = jnp.where(hit & (seen == lanes % SLOTS), local[i, s], wants)
        seen = seen + hit.astype(jnp.int32)
        ranks = ranks + ((owners == name) & (lanes > e)).astype(jnp.int32)
        return wants, seen, ranks

    wants, _, ranks = lax.fori_loop(
        0, BLOCKS * SLOTS, rank_entry, (nothing, nothing, nothing)
    )
    wants_v[...] = wants
    from_x = (x - owners // SIDE + SIDE) % SIDE
    from_z = (z - owners % SIDE + SIDE) % SIDE
    index = nothing
    for q in range(QUARTERS):
        u, v = (from_x, from_z) if q % 2 == 0 else (from_z, from_x)
        if q // 2 == 1:
            u, v = (SIDE - u) % SIDE, (SIDE - v) % SIDE
        leaf = nothing
        for a, b in LEAVES:
            leaf = leaf + (u * SIDE + v == a * SIDE + b).astype(jnp.int32)
        at = owners * BLOCKS + locals_ + leaf * (ranks - locals_)
        at = jnp.where(lanes % SLOTS < counts, at, ZERO)
        index = jnp.where(subs == q, at, index)
    index_v[...] = index
    index_copy = pltpu.make_async_copy(index_v, index_s, table_sem.at[0])
    index_copy.start()

    tell = [
        pltpu.make_async_remote_copy(
            src_ref=wants_v,
            dst_ref=wants_in.at[side],
            send_sem=wants_send.at[side],
            recv_sem=wants_recv.at[side],
            device_id=(neighbour, grp),
            device_id_type=MESH,
        )
        for neighbour, side in around
    ]
    for one in tell:
        one.start()

    for panel in panels_a + panels_b:
        panel[:, ZERO] = jnp.zeros((QUARTERS, TALL, WIDE), BF16)
    clear_a0()
    clear_a1()
    clear_b0()
    clear_b1()
    for one in tell:
        one.wait()
    wants_copy = pltpu.make_async_copy(wants_in, wants_s, table_sem.at[1])
    wants_copy.start()
    wants_copy.wait()
    index_copy.wait()

    def band_part(panel, edges):
        for copy in edges:
            copy.wait()

        @pl.loop(0, BLOCKS)
        def _(i):
            acc[i] = near(panel, i, both)

    edges_b = []

    def first_half(h, send_half):
        @pl.loop(0, BLOCKS)
        def _(i):
            total = long_range(panels_a, i, (h,), acc[i, :, pl.ds(h * WIDE, WIDE)])
            value = total.astype(BF16)
            for q in range(QUARTERS):
                panels_b[h][q, own + i] = value[q * TALL : (q + 1) * TALL]

        send_half()
        copies = halo(1, panels_b[h], h)
        for copy in copies:
            copy.start()
        edges_b.extend(copies)

    pass_a0(0)
    pass_a1(0)
    load_band.wait()
    band_part(panels_a, edges_a)
    pass_a0(1)
    pass_a0(2)
    pass_a1(1)
    pass_a0(3)
    pass_a1(2)
    load_far.wait()
    collect_a0()
    first_half(0, own_b0)
    pass_a1(3)
    sent_a0()
    pass_b0(0)
    pass_b0(1)
    collect_a1()
    first_half(1, own_b1)
    sent_a1()
    pass_b1(0)
    band_part(panels_b, edges_b)
    pass_b0(2)
    pass_b1(1)
    pass_b0(3)
    pass_b1(2)
    collect_b0()

    def add_long_range(i, h):
        columns = pl.ds(h * WIDE, WIDE)
        acc[i, :, columns] = long_range(panels_b, i, (h,), acc[i, :, columns])

    @pl.loop(0, BLOCKS)
    def _(i):
        add_long_range(i, 0)

    pass_b1(3)
    collect_b1()

    gram_v[...] = jnp.zeros((B, B), F32)
    gram_c[...] = jnp.zeros((B, B), F32)

    def add_gram(block):
        top = block.astype(BF16)
        rest = block - top.astype(F32)
        middle = rest.astype(BF16)
        low = (rest - middle.astype(F32)).astype(BF16)
        top_t = top.T
        gram_v[...] += dot(top_t, top) + dot(middle.T, middle)
        gram_c[...] += dot(top_t, middle) + dot(top_t, low)

    add_long_range(0, 1)

    @pl.loop(1, BLOCKS)
    def _(i):
        done = acc[i - 1]
        columns = pl.ds(WIDE, WIDE)
        total = long_range(panels_b, i, (1,), acc[i, :, columns])
        add_gram(done)
        acc[i, :, columns] = total

    add_gram(acc[BLOCKS - 1])
    store = pltpu.make_async_copy(acc, second_out, out_sem.at[0])
    store.start()
    cross = gram_c[...]
    whole = gram_v[...] + cross + cross.T
    corner[: B // 2] = whole[: B // 2, : B // 2]
    corner[B // 2 : B] = whole[B // 2 :, : B // 2]
    corner[B:] = whole[B // 2 :, B // 2 :]

    def scatter(k):
        to = (row + k) % N_ROW
        return pltpu.make_async_remote_copy(
            src_ref=corner.at[pl.ds(to * PART, PART)],
            dst_ref=parts.at[row],
            send_sem=scatter_send.at[k],
            recv_sem=scatter_recv.at[k],
            device_id=(to, grp),
            device_id_type=MESH,
        )

    @pl.loop(1, N_ROW)
    def _(k):
        scatter(k).start()

    parts[row] = corner[pl.ds(row * PART, PART)]

    @pl.loop(1, N_ROW)
    def _(k):
        origin = (row + N_ROW - k) % N_ROW
        pltpu.make_async_copy(parts.at[origin], parts.at[origin], scatter_recv.at[k]).wait()

    total = parts[0]
    for k in range(1, N_ROW):
        total = total + parts[k]
    shares[y] = total

    def share(k):
        return pltpu.make_async_remote_copy(
            src_ref=shares.at[y],
            dst_ref=shares.at[y],
            send_sem=share_send.at[k],
            recv_sem=share_recv.at[k],
            device_id=(row, along(k)),
            device_id_type=MESH,
        )

    for k in range(1, SIDE):
        share(k).start()
    for k in range(1, SIDE):
        origin = (y + SIDE - k) % SIDE
        pltpu.make_async_copy(shares.at[origin], shares.at[origin], share_recv.at[k]).wait()
    pair[0] = (shares[0] + shares[1]) + (shares[2] + shares[3])
    swap = pltpu.make_async_remote_copy(
        src_ref=pair.at[0],
        dst_ref=pair.at[1],
        send_sem=share_send.at[0],
        recv_sem=share_recv.at[0],
        device_id=(row, y * 2 + 1 - core),
        device_id_type=MESH,
    )
    swap.start()
    swap.wait()
    total = pair[0] + pair[1]
    summed[pl.ds(row * PART, PART)] = total

    def spread(k):
        mine = pl.ds(row * PART, PART)
        return pltpu.make_async_remote_copy(
            src_ref=summed.at[mine],
            dst_ref=summed.at[mine],
            send_sem=spread_send.at[k],
            recv_sem=spread_recv.at[k],
            device_id=((row + k) % N_ROW, grp),
            device_id_type=MESH,
        )

    @pl.loop(1, N_ROW)
    def _(k):
        spread(k).start()

    @pl.loop(1, N_ROW)
    def _(k):
        theirs = pl.ds(((row + N_ROW - k) % N_ROW) * PART, PART)
        pltpu.make_async_copy(summed.at[theirs], summed.at[theirs], spread_recv.at[k]).wait()

    finish = pltpu.make_async_copy(summed, gram_out, out_sem.at[1])
    finish.start()

    @pl.loop(1, N_ROW)
    def _(k):
        scatter(k).wait_send()
        spread(k).wait_send()

    for k in range(1, SIDE):
        share(k).wait_send()

    sent_b0()
    sent_b1()
    store.wait()
    finish.wait()


def factor_kernel(gram, second, basis, factor, m, inv_v, second_v, out_v, sem):
    load = pltpu.make_async_copy(second, second_v, sem.at[0])
    load.start()
    tile = (SUB, LANE)
    halves = range(B // LANE)
    lanes = lax.broadcasted_iota(jnp.int32, tile, 1)
    subs = lax.broadcasted_iota(jnp.int32, tile, 0)
    m[: B // 2, : B // 2] = gram[: B // 2]
    m[B // 2 :, : B // 2] = gram[B // 2 : B]
    m[: B // 2, B // 2 :] = gram[B // 2 : B].T
    m[B // 2 :, B // 2 :] = gram[B:]

    def row_of(a, r):
        return jnp.broadcast_to(a[r : r + 1, :], tile)

    def column_of(a, c):
        return jnp.broadcast_to(a[:, c : c + 1], tile)

    def at(i, l):
        return (pl.ds(i * SUB, SUB), pl.ds(l * LANE, LANE))

    for g in range(B // SUB):
        home, first = g * SUB // LANE, g * SUB % LANE
        inside = (lanes >= first) & (lanes < first + SUB)
        pivot = [m[at(g, l)] for l in halves]
        columns = [column_of(pivot[home], first + c) for c in range(SUB)]
        s = {(r, c): row_of(columns[c], r) for c in range(SUB) for r in range(c, SUB)}
        roots, ratios = [], {}
        for j in range(SUB):
            d = s[j, j]
            inverse = 1.0 / d
            roots.append(lax.rsqrt(d))
            old = {r: s[max(r, j), min(r, j)] for r in range(SUB) if r != j}
            new = {r: old[r] * inverse for r in old}
            for r in old:
                for c in old:
                    if c <= r:
                        s[r, c] = s[r, c] - old[r] * new[c]
            for r in old:
                s[max(r, j), min(r, j)] = new[r]
                if r > j:
                    ratios[r, j] = new[r]
            s[j, j] = -inverse
        unit = jnp.where(inside, (lanes - first == subs).astype(F32), pivot[home])
        source = [unit if l == home else pivot[l] for l in halves]
        rows = [[row_of(source[l], r) for l in halves] for r in range(SUB)]
        weights = []
        for c in range(SUB):
            per = []
            for l in halves:
                terms = [s[max(r, c), min(r, c)] * rows[r][l] for r in range(SUB)]
                while len(terms) > 1:
                    terms = [terms[k] + terms[k + 1] for k in range(0, len(terms), 2)]
                per.append(terms[0])
            weights.append(per)
        for i in range(g + 1, B // SUB):
            left = m[at(i, home)]
            columns = [column_of(left, first + c) for c in range(SUB)]
            for l in halves:
                value = jnp.where(inside, 0.0, left) if l == home else m[at(i, l)]
                terms = [columns[c] * weights[c][l] for c in range(SUB)]
                while len(terms) > 1:
                    terms = [terms[k] + terms[k + 1] for k in range(0, len(terms), 2)]
                m[at(i, l)] = value + terms[0]
        upper = [row_of(pivot[home], r) for r in range(SUB)]
        inv_tiles = [jnp.zeros(tile, F32) for _ in halves]
        fac_tiles = [jnp.zeros(tile, F32) for _ in halves]
        for r in range(SUB):
            for j in range(r):
                upper[r] = upper[r] - ratios[r, j] * upper[j]
                for l in halves:
                    rows[r][l] = rows[r][l] - ratios[r, j] * rows[j][l]
            here = subs == r
            for l in halves:
                if l <= home:
                    inv_tiles[l] = jnp.where(here, rows[r][l] * roots[r], inv_tiles[l])
                if l > home:
                    fac_tiles[l] = jnp.where(here, rows[r][l] * roots[r], fac_tiles[l])
                if l == home:
                    fac_tiles[l] = jnp.where(here, upper[r] * roots[r], fac_tiles[l])
        inv_tiles[home] = jnp.where(lanes < first + SUB, inv_tiles[home], 0.0)
        fac_tiles[home] = jnp.where(lanes - first >= subs, fac_tiles[home], 0.0)
        for l in halves:
            inv_v[at(g, l)] = inv_tiles[l] * SCALE
            factor[at(g, l)] = fac_tiles[l] * (1.0 / SCALE)

    turned = inv_v[...].T
    top = turned.astype(BF16)
    rest = (turned - top.astype(F32)).astype(BF16)
    load.wait()

    def store(i):
        return pltpu.make_async_copy(out_v.at[i], basis.at[i], sem.at[1 + i])

    @pl.loop(0, BLOCKS)
    def _(i):
        x = second_v[i]
        x_top = x.astype(BF16)
        x_rest = (x - x_top.astype(F32)).astype(BF16)
        out_v[i] = dot(x_top, top) + (dot(x_top, rest) + dot(x_rest, top))
        store(i).start()

    @pl.loop(0, BLOCKS)
    def _(i):
        store(i).wait()


def power_step(sketch, band_tiles, far_tiles, far_owner, far_local, far_count):
    any_space = pl.BlockSpec(memory_space=pl.ANY)
    dma = pltpu.SemaphoreType.DMA
    return pl.pallas_call(
        range_kernel,
        out_shape=(
            jax.ShapeDtypeStruct((BLOCKS, B, B), F32),
            jax.ShapeDtypeStruct((TRI, B // 2), F32),
        ),
        in_specs=[any_space] * 6,
        out_specs=(any_space, any_space),
        scratch_shapes=[
            pltpu.VMEM((QUARTERS, N_PANEL + 3, TALL, WIDE), BF16),
            pltpu.VMEM((QUARTERS, N_PANEL + 3, TALL, WIDE), BF16),
            pltpu.VMEM((QUARTERS, N_PANEL + 3, TALL, WIDE), BF16),
            pltpu.VMEM((QUARTERS, N_PANEL + 3, TALL, WIDE), BF16),
            pltpu.VMEM((BLOCKS, 3, B, B), BF16),
            pltpu.VMEM((BLOCKS, SLOTS, B, B), BF16),
            pltpu.VMEM((BLOCKS, B, B), F32),
            pltpu.VMEM((UNITS, len(LEAVES), CAP, TALL, WIDE), BF16),
            pltpu.VMEM((B, B), F32),
            pltpu.VMEM((B, B), F32),
            pltpu.VMEM((TRI, B // 2), F32),
            pltpu.VMEM((TRI, B // 2), F32),
            pltpu.VMEM((N_ROW, PART, B // 2), F32),
            pltpu.VMEM((SIDE, PART, B // 2), F32),
            pltpu.VMEM((2, PART, B // 2), F32),
            pltpu.VMEM((8, 128), jnp.int32),
            pltpu.VMEM((4, 8, 128), jnp.int32),
            pltpu.VMEM((8, 128), jnp.int32),
            pltpu.SMEM((4, 8, 128), jnp.int32),
            pltpu.SMEM((8, 128), jnp.int32),
            pltpu.SMEM((BLOCKS, SLOTS), jnp.int32),
            pltpu.SMEM((BLOCKS, SLOTS), jnp.int32),
            pltpu.SMEM((BLOCKS,), jnp.int32),
            dma((5 + UNITS,)),
            dma((2, UNITS, N_ROW)),
            dma((2, UNITS)),
            dma((2, 4)),
            dma((2, 4)),
            dma((4,)),
            dma((4,)),
            dma((2,)),
            dma((N_ROW,)),
            dma((N_ROW,)),
            dma((SIDE,)),
            dma((SIDE,)),
            dma((N_ROW,)),
            dma((N_ROW,)),
            dma((2,)),
        ],
        compiler_params=pltpu.CompilerParams(
            collective_id=0, has_side_effects=True, vmem_limit_bytes=58 * 1024 * 1024
        ),
        cost_estimate=pl.CostEstimate(
            flops=4 * 88 * B**3, bytes_accessed=15 << 20, transcendentals=0
        ),
    )(sketch, band_tiles, far_tiles, far_owner, far_local, far_count)


def orthonormalize(gram, second):
    whole = pl.BlockSpec(memory_space=pltpu.VMEM)
    any_space = pl.BlockSpec(memory_space=pl.ANY)
    return pl.pallas_call(
        factor_kernel,
        out_shape=(
            jax.ShapeDtypeStruct((BLOCKS, B, B), F32),
            jax.ShapeDtypeStruct((B, B), F32),
        ),
        in_specs=[whole, any_space],
        out_specs=(any_space, whole),
        scratch_shapes=[
            pltpu.VMEM((B, B), F32),
            pltpu.VMEM((B, B), F32),
            pltpu.VMEM((BLOCKS, B, B), F32),
            pltpu.VMEM((BLOCKS, B, B), F32),
            pltpu.SemaphoreType.DMA((1 + BLOCKS,)),
        ],
        compiler_params=pltpu.CompilerParams(vmem_limit_bytes=58 * 1024 * 1024),
    )(gram, second)


def body(sketch, band_tiles, far_tiles, far_owner, far_local, far_count):
    second, gram = power_step(sketch, band_tiles, far_tiles, far_owner, far_local, far_count)
    return orthonormalize(gram, second)


def solution(mesh):
    in_specs = (
        P(("row", "grp"), None, None),
        P(("row", "grp"), None, None, None),
        P(("row", "grp"), None, None, None),
        P(("row", "grp"), None),
        P(("row", "grp"), None),
        P(("row", "grp")),
    )
    out_specs = (P(("row", "grp"), None, None), P())
    return jax.shard_map(body, mesh=mesh, in_specs=in_specs, out_specs=out_specs, check_vma=False)
```

```python
import math

import jax
import jax.numpy as jnp
from jax import lax
from jax.experimental import pallas as pl
from jax.experimental.pallas import tpu as pltpu
from jax.sharding import PartitionSpec as P

MESH = pl.DeviceIdType.MESH
SIDE = 4
N_ROW = SIDE * SIDE
N_GRP = 8
BLOCKS = 8
SLOTS = 8
B = 256
N_PANEL = N_ROW * BLOCKS
ZERO, LEFT, RIGHT = N_PANEL, N_PANEL + 1, N_PANEL + 2
TRI = 3 * B // 2
PART = TRI // N_ROW
CAP = 6
QUARTERS = 4
UNITS = 8
TALL, WIDE = B // 4, B // 2
TREE = (
    (((0, 0), ((1, 0), (0, 1), (-1, 0), (0, -1))),),
    (((1, 0), ((1, 0), (0, 1), (0, -1))), ((0, 1), ((0, 1), (-1, 0)))),
    (((2, 0), ((0, -1), (0, 1))), ((0, 2), ((1, 0), (-1, 0)))),
    (((2, 3), ((0, -1), (1, 0))),),
)
INNER = [node for level in TREE for node, _ in level]
LEAVES = [(u, v) for u in range(SIDE) for v in range(SIDE) if (u, v) not in INNER]
F32 = jnp.float32
BF16 = jnp.bfloat16
SUB, LANE = 8, 128
SCALE = math.sqrt(BLOCKS * B * N_ROW * N_GRP)


def dot(a, b):
    return jnp.dot(a, b, preferred_element_type=F32)


def range_kernel(
    sketch, band, far, owner_in, local_in, count_in,
    second_out, gram_out,
    panel_a0, panel_a1, panel_b0, panel_b1, band_v, far_v, acc, packed, gram_v, gram_c, corner, summed, parts, shares, pair,
    wants_v, wants_in, index_v, wants_s, index_s, owner, local, count,
    load_sem, recv_sem, send_sem, halo_send, halo_recv, wants_send, wants_recv, table_sem,
    scatter_send, scatter_recv, share_send, share_recv, spread_send, spread_recv, out_sem,
):
    row, grp = lax.axis_index("row"), lax.axis_index("grp")
    x, z = row // SIDE, row % SIDE
    device = row * N_GRP + grp
    after, before = (device + 1) % (N_ROW * N_GRP), (device + N_ROW * N_GRP - 1) % (N_ROW * N_GRP)
    after_id = (after // N_GRP, after % N_GRP)
    before_id = (before // N_GRP, before % N_GRP)
    own = row * BLOCKS
    panels_a, panels_b = (panel_a0, panel_a1), (panel_b0, panel_b1)
    y, core = grp // 2, grp % 2
    around = (
        ((x + 1) % SIDE * SIDE + z, 1),
        ((x + SIDE - 1) % SIDE * SIDE + z, 0),
        (x * SIDE + (z + 1) % SIDE, 3),
        (x * SIDE + (z + SIDE - 1) % SIDE, 2),
    )

    def along(k):
        return (y + k) % SIDE * 2 + core


    def load_unit(n):
        h, q = n // QUARTERS, n % QUARTERS
        return pltpu.make_async_copy(
            sketch.at[:, pl.ds(q * TALL, TALL), pl.ds(h * WIDE, WIDE)],
            panels_a[h].at[q, pl.ds(own, BLOCKS)],
            load_sem.at[2 + n],
        )

    barrier = pltpu.get_barrier_semaphore()

    def greet(device_id):
        pl.semaphore_signal(barrier, inc=1, device_id=device_id, device_id_type=MESH)

    for neighbour, _ in around:
        greet((neighbour, grp))
    greet(after_id)
    greet(before_id)
    for k in range(1, SIDE):
        greet((row, along(k)))

    load_band = pltpu.make_async_copy(band, band_v, load_sem.at[0])
    load_far = pltpu.make_async_copy(far, far_v, load_sem.at[1])
    for n in range(UNITS):
        load_unit(n).start()
    load_scalars = [
        pltpu.make_async_copy(source, target, load_sem.at[2 + UNITS + k])
        for k, (source, target) in enumerate(
            ((owner_in, owner), (local_in, local), (count_in, count))
        )
    ]
    for one in load_scalars:
        one.start()
    load_band.start()
    load_far.start()

    for n in range(UNITS):
        load_unit(n).wait()
    pl.semaphore_wait(barrier, len(around) + 2 + SIDE - 1)

    def gather_steps(app, h, panel):
        base = h * QUARTERS

        def turn(n):
            return n % 2, 1 - 2 * ((n // 2) % 2)

        def place(n, first, second):
            swap, sign = turn(n)
            to_x = (x + 2 * SIDE + sign * (first * (1 - swap) + second * swap)) % SIDE
            to_z = (z + 2 * SIDE + sign * (first * swap + second * (1 - swap))) % SIDE
            return to_x * SIDE + to_z

        def send(n, u, v, first, second):
            slots = pl.ds(place(n, -u, -v) * BLOCKS, BLOCKS)
            to_u, to_v = (u + first) % SIDE, (v + second) % SIDE
            pltpu.make_async_remote_copy(
                src_ref=panel.at[n, slots],
                dst_ref=panel.at[n, slots],
                send_sem=send_sem.at[app, base + n],
                recv_sem=recv_sem.at[app, base + n, to_u * SIDE + to_v],
                device_id=(place(n, first, second), grp),
                device_id_type=MESH,
            ).start()

        def send_leaf(n, u, v, first, second):
            swap, sign = turn(n)
            side = 2 * (swap if first else 1 - swap) + (1 - (first + second) * sign) // 2
            source = place(n, -u, -v)
            to = ((u + first) % SIDE, (v + second) % SIDE)
            leaf = LEAVES.index(to)
            blocks = [panel[n, source * BLOCKS + b] for b in range(BLOCKS)]
            for k in range(CAP):
                wanted = wants_s[side, 0, source * SLOTS + k]
                out = blocks[0]
                for b in range(1, BLOCKS):
                    out = jnp.where(wanted == b, blocks[b], out)
                packed[base + n, leaf, k] = out
            pltpu.make_async_remote_copy(
                src_ref=packed.at[base + n, leaf],
                dst_ref=panel.at[n, pl.ds(source * BLOCKS, CAP)],
                send_sem=send_sem.at[app, base + n],
                recv_sem=recv_sem.at[app, base + n, to[0] * SIDE + to[1]],
                device_id=(place(n, first, second), grp),
                device_id_type=MESH,
            ).start()

        def arrived(n, u, v):
            slots = pl.ds(place(n, -u, -v) * BLOCKS, CAP if (u, v) in LEAVES else BLOCKS)
            pltpu.make_async_copy(
                panel.at[n, slots], panel.at[n, slots], recv_sem.at[app, base + n, u * SIDE + v]
            ).wait()

        def edges_of(n, node, steps, leaves):
            for first, second in steps:
                to = ((node[0] + first) % SIDE, (node[1] + second) % SIDE)
                if (to in LEAVES) == leaves:
                    (send_leaf if leaves else send)(n, *node, first, second)

        def each(step):
            return lambda: pl.loop(0, QUARTERS)(step)

        def pass_on(depth):
            def step(n):
                for node, steps in TREE[depth]:
                    if depth:
                        arrived(n, *node)
                        edges_of(n, node, steps, False)
                    edges_of(n, node, steps, True)

            pl.loop(0, QUARTERS)(step)

        @each
        def send_own(n):
            edges_of(n, *TREE[0][0], False)

        @each
        def collect(n):
            for node in LEAVES:
                arrived(n, *node)

        @each
        def clear(n):
            for u, v in LEAVES:
                for k in range(CAP, BLOCKS):
                    panel[n, place(n, -u, -v) * BLOCKS + k] = jnp.zeros((TALL, WIDE), BF16)

        @each
        def sent(n):
            total = (len(INNER) - 1) * BLOCKS + len(LEAVES) * CAP
            pltpu.make_async_copy(
                panel.at[n, pl.ds(0, total)],
                panel.at[n, pl.ds(0, total)],
                send_sem.at[app, base + n],
            ).wait()

        return send_own, pass_on, collect, clear, sent

    def halo(app, panel, h):
        units = pl.ds(0, QUARTERS)
        tail = pltpu.make_async_remote_copy(
            src_ref=panel.at[units, own + BLOCKS - 1],
            dst_ref=panel.at[units, LEFT],
            send_sem=halo_send.at[app, 2 * h],
            recv_sem=halo_recv.at[app, 2 * h],
            device_id=after_id,
            device_id_type=MESH,
        )
        head = pltpu.make_async_remote_copy(
            src_ref=panel.at[units, own],
            dst_ref=panel.at[units, RIGHT],
            send_sem=halo_send.at[app, 2 * h + 1],
            recv_sem=halo_recv.at[app, 2 * h + 1],
            device_id=before_id,
            device_id_type=MESH,
        )
        return head, tail

    def column(panel, at):
        return jnp.concatenate([panel[q, at(q)] for q in range(QUARTERS)], axis=0)

    def block_of(panels, halves, at):
        return jnp.concatenate([column(panels[h], at) for h in halves], axis=1)

    def near(panel, i, halves):
        left = jnp.where(i == 0, jnp.where(device == 0, ZERO, LEFT), own + i - 1)
        right = jnp.where(
            i == BLOCKS - 1,
            jnp.where(device == N_ROW * N_GRP - 1, ZERO, RIGHT),
            own + i + 1,
        )
        return (
            dot(band_v[i, 0], block_of(panel, halves, lambda q: left))
            + dot(band_v[i, 1], block_of(panel, halves, lambda q: own + i))
            + dot(band_v[i, 2], block_of(panel, halves, lambda q: right))
        )

    def long_range(panel, i, halves, total):
        for s in range(SLOTS):
            remote = block_of(panel, halves, lambda q: index_s[q, i * SLOTS + s])
            total = total + dot(far_v[i, s], remote)
        return total

    both = (0, 1)
    gathers = [
        [gather_steps(app, h, panels[h]) for h in both]
        for app, panels in enumerate((panels_a, panels_b))
    ]
    (own_a0, pass_a0, collect_a0, clear_a0, sent_a0), (
        own_a1, pass_a1, collect_a1, clear_a1, sent_a1
    ) = gathers[0]
    (own_b0, pass_b0, collect_b0, clear_b0, sent_b0), (
        own_b1, pass_b1, collect_b1, clear_b1, sent_b1
    ) = gathers[1]

    own_a0()
    own_a1()
    edges_a = [copy for h in both for copy in halo(0, panels_a[h], h)]
    for copy in edges_a:
        copy.start()
    for one in load_scalars:
        one.wait()
    table = (8, 128)
    lanes = lax.broadcasted_iota(jnp.int32, table, 1)
    subs = lax.broadcasted_iota(jnp.int32, table, 0)
    nothing = jnp.zeros(table, jnp.int32)

    def spread_entry(e, carry):
        owners, locals_, counts = carry
        i, s = e // SLOTS, e % SLOTS
        here = lanes == e
        return (
            jnp.where(here, owner[i, s], owners),
            jnp.where(here, local[i, s], locals_),
            jnp.where(here, count[i], counts),
        )

    owners, locals_, counts = lax.fori_loop(
        0, BLOCKS * SLOTS, spread_entry, (nothing, nothing, nothing)
    )

    def rank_entry(e, carry):
        wants, seen, ranks = carry
        i, s = e // SLOTS, e % SLOTS
        name = owner[i, s]
        hit = (lanes // SLOTS) == name
        wants = jnp.where(hit & (seen == lanes % SLOTS), local[i, s], wants)
        seen = seen + hit.astype(jnp.int32)
        ranks = ranks + ((owners == name) & (lanes > e)).astype(jnp.int32)
        return wants, seen, ranks

    wants, _, ranks = lax.fori_loop(
        0, BLOCKS * SLOTS, rank_entry, (nothing, nothing, nothing)
    )
    wants_v[...] = wants
    from_x = (x - owners // SIDE + SIDE) % SIDE
    from_z = (z - owners % SIDE + SIDE) % SIDE
    index = nothing
    for q in range(QUARTERS):
        u, v = (from_x, from_z) if q % 2 == 0 else (from_z, from_x)
        if q // 2 == 1:
            u, v = (SIDE - u) % SIDE, (SIDE - v) % SIDE
        leaf = nothing
        for a, b in LEAVES:
            leaf = leaf + (u * SIDE + v == a * SIDE + b).astype(jnp.int32)
        at = owners * BLOCKS + locals_ + leaf * (ranks - locals_)
        at = jnp.where(lanes % SLOTS < counts, at, ZERO)
        index = jnp.where(subs == q, at, index)
    index_v[...] = index
    index_copy = pltpu.make_async_copy(index_v, index_s, table_sem.at[0])
    index_copy.start()

    tell = [
        pltpu.make_async_remote_copy(
            src_ref=wants_v,
            dst_ref=wants_in.at[side],
            send_sem=wants_send.at[side],
            recv_sem=wants_recv.at[side],
            device_id=(neighbour, grp),
            device_id_type=MESH,
        )
        for neighbour, side in around
    ]
    for one in tell:
        one.start()

    for panel in panels_a + panels_b:
        panel[:, ZERO] = jnp.zeros((QUARTERS, TALL, WIDE), BF16)
    clear_a0()
    clear_a1()
    clear_b0()
    clear_b1()
    for one in tell:
        one.wait()
    wants_copy = pltpu.make_async_copy(wants_in, wants_s, table_sem.at[1])
    wants_copy.start()
    wants_copy.wait()
    index_copy.wait()

    def band_part(panel, edges):
        for copy in edges:
            copy.wait()

        @pl.loop(0, BLOCKS)
        def _(i):
            acc[i] = near(panel, i, both)

    edges_b = []

    def first_half(h, send_half):
        @pl.loop(0, BLOCKS)
        def _(i):
            total = long_range(panels_a, i, (h,), acc[i, :, pl.ds(h * WIDE, WIDE)])
            value = total.astype(BF16)
            for q in range(QUARTERS):
                panels_b[h][q, own + i] = value[q * TALL : (q + 1) * TALL]

        send_half()
        copies = halo(1, panels_b[h], h)
        for copy in copies:
            copy.start()
        edges_b.extend(copies)

    pass_a0(0)
    pass_a1(0)
    load_band.wait()
    band_part(panels_a, edges_a)
    pass_a0(1)
    pass_a0(2)
    pass_a1(1)
    pass_a0(3)
    pass_a1(2)
    load_far.wait()
    collect_a0()
    first_half(0, own_b0)
    pass_a1(3)
    sent_a0()
    pass_b0(0)
    pass_b0(1)
    collect_a1()
    first_half(1, own_b1)
    sent_a1()
    pass_b1(0)
    band_part(panels_b, edges_b)
    pass_b0(2)
    pass_b1(1)
    pass_b0(3)
    pass_b1(2)
    collect_b0()

    def add_long_range(i, h):
        columns = pl.ds(h * WIDE, WIDE)
        acc[i, :, columns] = long_range(panels_b, i, (h,), acc[i, :, columns])

    @pl.loop(0, BLOCKS)
    def _(i):
        add_long_range(i, 0)

    pass_b1(3)
    collect_b1()

    gram_v[...] = jnp.zeros((B, B), F32)
    gram_c[...] = jnp.zeros((B, B), F32)

    def add_gram(block):
        top = block.astype(BF16)
        rest = block - top.astype(F32)
        middle = rest.astype(BF16)
        low = (rest - middle.astype(F32)).astype(BF16)
        top_t = top.T
        gram_v[...] += dot(top_t, top) + dot(middle.T, middle)
        gram_c[...] += dot(top_t, middle) + dot(top_t, low)

    add_long_range(0, 1)

    @pl.loop(1, BLOCKS)
    def _(i):
        done = acc[i - 1]
        columns = pl.ds(WIDE, WIDE)
        total = long_range(panels_b, i, (1,), acc[i, :, columns])
        add_gram(done)
        acc[i, :, columns] = total

    add_gram(acc[BLOCKS - 1])
    store = pltpu.make_async_copy(acc, second_out, out_sem.at[0])
    store.start()
    cross = gram_c[...]
    whole = gram_v[...] + cross + cross.T
    corner[: B // 2] = whole[: B // 2, : B // 2]
    corner[B // 2 : B] = whole[B // 2 :, : B // 2]
    corner[B:] = whole[B // 2 :, B // 2 :]

    def scatter(k):
        to = (row + k) % N_ROW
        return pltpu.make_async_remote_copy(
            src_ref=corner.at[pl.ds(to * PART, PART)],
            dst_ref=parts.at[row],
            send_sem=scatter_send.at[k],
            recv_sem=scatter_recv.at[k],
            device_id=(to, grp),
            device_id_type=MESH,
        )

    @pl.loop(1, N_ROW)
    def _(k):
        scatter(k).start()

    parts[row] = corner[pl.ds(row * PART, PART)]

    @pl.loop(1, N_ROW)
    def _(k):
        origin = (row + N_ROW - k) % N_ROW
        pltpu.make_async_copy(parts.at[origin], parts.at[origin], scatter_recv.at[k]).wait()

    total = parts[0]
    for k in range(1, N_ROW):
        total = total + parts[k]
    shares[y] = total

    def share(k):
        return pltpu.make_async_remote_copy(
            src_ref=shares.at[y],
            dst_ref=shares.at[y],
            send_sem=share_send.at[k],
            recv_sem=share_recv.at[k],
            device_id=(row, along(k)),
            device_id_type=MESH,
        )

    for k in range(1, SIDE):
        share(k).start()
    for k in range(1, SIDE):
        origin = (y + SIDE - k) % SIDE
        pltpu.make_async_copy(shares.at[origin], shares.at[origin], share_recv.at[k]).wait()
    pair[0] = (shares[0] + shares[1]) + (shares[2] + shares[3])
    swap = pltpu.make_async_remote_copy(
        src_ref=pair.at[0],
        dst_ref=pair.at[1],
        send_sem=share_send.at[0],
        recv_sem=share_recv.at[0],
        device_id=(row, y * 2 + 1 - core),
        device_id_type=MESH,
    )
    swap.start()
    swap.wait()
    total = pair[0] + pair[1]
    summed[pl.ds(row * PART, PART)] = total

    def spread(k):
        mine = pl.ds(row * PART, PART)
        return pltpu.make_async_remote_copy(
            src_ref=summed.at[mine],
            dst_ref=summed.at[mine],
            send_sem=spread_send.at[k],
            recv_sem=spread_recv.at[k],
            device_id=((row + k) % N_ROW, grp),
            device_id_type=MESH,
        )

    @pl.loop(1, N_ROW)
    def _(k):
        spread(k).start()

    @pl.loop(1, N_ROW)
    def _(k):
        theirs = pl.ds(((row + N_ROW - k) % N_ROW) * PART, PART)
        pltpu.make_async_copy(summed.at[theirs], summed.at[theirs], spread_recv.at[k]).wait()

    finish = pltpu.make_async_copy(summed, gram_out, out_sem.at[1])
    finish.start()

    @pl.loop(1, N_ROW)
    def _(k):
        scatter(k).wait_send()
        spread(k).wait_send()

    for k in range(1, SIDE):
        share(k).wait_send()

    sent_b0()
    sent_b1()
    store.wait()
    finish.wait()


def factor_kernel(gram, second, basis, factor, m, inv_v, second_v, out_v, sem):
    load = pltpu.make_async_copy(second, second_v, sem.at[0])
    load.start()
    tile = (SUB, LANE)
    halves = range(B // LANE)
    lanes = lax.broadcasted_iota(jnp.int32, tile, 1)
    subs = lax.broadcasted_iota(jnp.int32, tile, 0)
    m[: B // 2, : B // 2] = gram[: B // 2]
    m[B // 2 :, : B // 2] = gram[B // 2 : B]
    m[: B // 2, B // 2 :] = gram[B // 2 : B].T
    m[B // 2 :, B // 2 :] = gram[B:]

    def row_of(a, r):
        return jnp.broadcast_to(a[r : r + 1, :], tile)

    def column_of(a, c):
        return jnp.broadcast_to(a[:, c : c + 1], tile)

    def at(i, l):
        return (pl.ds(i * SUB, SUB), pl.ds(l * LANE, LANE))

    for g in range(B // SUB):
        home, first = g * SUB // LANE, g * SUB % LANE
        inside = (lanes >= first) & (lanes < first + SUB)
        pivot = [m[at(g, l)] for l in halves]
        columns = [column_of(pivot[home], first + c) for c in range(SUB)]
        s = {(r, c): row_of(columns[c], r) for c in range(SUB) for r in range(c, SUB)}
        roots, ratios = [], {}
        for j in range(SUB):
            d = s[j, j]
            inverse = 1.0 / d
            roots.append(lax.rsqrt(d))
            old = {r: s[max(r, j), min(r, j)] for r in range(SUB) if r != j}
            new = {r: old[r] * inverse for r in old}
            for r in old:
                for c in old:
                    if c <= r:
                        s[r, c] = s[r, c] - old[r] * new[c]
            for r in old:
                s[max(r, j), min(r, j)] = new[r]
                if r > j:
                    ratios[r, j] = new[r]
            s[j, j] = -inverse
        unit = jnp.where(inside, (lanes - first == subs).astype(F32), pivot[home])
        source = [unit if l == home else pivot[l] for l in halves]
        rows = [[row_of(source[l], r) for l in halves] for r in range(SUB)]
        weights = []
        for c in range(SUB):
            per = []
            for l in halves:
                terms = [s[max(r, c), min(r, c)] * rows[r][l] for r in range(SUB)]
                while len(terms) > 1:
                    terms = [terms[k] + terms[k + 1] for k in range(0, len(terms), 2)]
                per.append(terms[0])
            weights.append(per)
        for i in range(g + 1, B // SUB):
            left = m[at(i, home)]
            columns = [column_of(left, first + c) for c in range(SUB)]
            for l in halves:
                value = jnp.where(inside, 0.0, left) if l == home else m[at(i, l)]
                terms = [columns[c] * weights[c][l] for c in range(SUB)]
                while len(terms) > 1:
                    terms = [terms[k] + terms[k + 1] for k in range(0, len(terms), 2)]
                m[at(i, l)] = value + terms[0]
        upper = [row_of(pivot[home], r) for r in range(SUB)]
        inv_tiles = [jnp.zeros(tile, F32) for _ in halves]
        fac_tiles = [jnp.zeros(tile, F32) for _ in halves]
        for r in range(SUB):
            for j in range(r):
                upper[r] = upper[r] - ratios[r, j] * upper[j]
                for l in halves:
                    rows[r][l] = rows[r][l] - ratios[r, j] * rows[j][l]
            here = subs == r
            for l in halves:
                if l <= home:
                    inv_tiles[l] = jnp.where(here, rows[r][l] * roots[r], inv_tiles[l])
                if l > home:
                    fac_tiles[l] = jnp.where(here, rows[r][l] * roots[r], fac_tiles[l])
                if l == home:
                    fac_tiles[l] = jnp.where(here, upper[r] * roots[r], fac_tiles[l])
        inv_tiles[home] = jnp.where(lanes < first + SUB, inv_tiles[home], 0.0)
        fac_tiles[home] = jnp.where(lanes - first >= subs, fac_tiles[home], 0.0)
        for l in halves:
            inv_v[at(g, l)] = inv_tiles[l] * SCALE
            factor[at(g, l)] = fac_tiles[l] * (1.0 / SCALE)

    turned = inv_v[...].T
    top = turned.astype(BF16)
    rest = (turned - top.astype(F32)).astype(BF16)
    load.wait()

    def store(i):
        return pltpu.make_async_copy(out_v.at[i], basis.at[i], sem.at[1 + i])

    for i in range(BLOCKS):
        x = second_v[i]
        x_top = x.astype(BF16)
        x_rest = (x - x_top.astype(F32)).astype(BF16)
        out_v[i] = dot(x_top, top) + (dot(x_top, rest) + dot(x_rest, top))
        store(i).start()

    @pl.loop(0, BLOCKS)
    def _(i):
        store(i).wait()


def power_step(sketch, band_tiles, far_tiles, far_owner, far_local, far_count):
    any_space = pl.BlockSpec(memory_space=pl.ANY)
    dma = pltpu.SemaphoreType.DMA
    return pl.pallas_call(
        range_kernel,
        out_shape=(
            jax.ShapeDtypeStruct((BLOCKS, B, B), F32),
            jax.ShapeDtypeStruct((TRI, B // 2), F32),
        ),
        in_specs=[any_space] * 6,
        out_specs=(any_space, any_space),
        scratch_shapes=[
            pltpu.VMEM((QUARTERS, N_PANEL + 3, TALL, WIDE), BF16),
            pltpu.VMEM((QUARTERS, N_PANEL + 3, TALL, WIDE), BF16),
            pltpu.VMEM((QUARTERS, N_PANEL + 3, TALL, WIDE), BF16),
            pltpu.VMEM((QUARTERS, N_PANEL + 3, TALL, WIDE), BF16),
            pltpu.VMEM((BLOCKS, 3, B, B), BF16),
            pltpu.VMEM((BLOCKS, SLOTS, B, B), BF16),
            pltpu.VMEM((BLOCKS, B, B), F32),
            pltpu.VMEM((UNITS, len(LEAVES), CAP, TALL, WIDE), BF16),
            pltpu.VMEM((B, B), F32),
            pltpu.VMEM((B, B), F32),
            pltpu.VMEM((TRI, B // 2), F32),
            pltpu.VMEM((TRI, B // 2), F32),
            pltpu.VMEM((N_ROW, PART, B // 2), F32),
            pltpu.VMEM((SIDE, PART, B // 2), F32),
            pltpu.VMEM((2, PART, B // 2), F32),
            pltpu.VMEM((8, 128), jnp.int32),
            pltpu.VMEM((4, 8, 128), jnp.int32),
            pltpu.VMEM((8, 128), jnp.int32),
            pltpu.SMEM((4, 8, 128), jnp.int32),
            pltpu.SMEM((8, 128), jnp.int32),
            pltpu.SMEM((BLOCKS, SLOTS), jnp.int32),
            pltpu.SMEM((BLOCKS, SLOTS), jnp.int32),
            pltpu.SMEM((BLOCKS,), jnp.int32),
            dma((5 + UNITS,)),
            dma((2, UNITS, N_ROW)),
            dma((2, UNITS)),
            dma((2, 4)),
            dma((2, 4)),
            dma((4,)),
            dma((4,)),
            dma((2,)),
            dma((N_ROW,)),
            dma((N_ROW,)),
            dma((SIDE,)),
            dma((SIDE,)),
            dma((N_ROW,)),
            dma((N_ROW,)),
            dma((2,)),
        ],
        compiler_params=pltpu.CompilerParams(
            collective_id=0, has_side_effects=True, vmem_limit_bytes=58 * 1024 * 1024
        ),
        cost_estimate=pl.CostEstimate(
            flops=4 * 88 * B**3, bytes_accessed=15 << 20, transcendentals=0
        ),
    )(sketch, band_tiles, far_tiles, far_owner, far_local, far_count)


def orthonormalize(gram, second):
    whole = pl.BlockSpec(memory_space=pltpu.VMEM)
    any_space = pl.BlockSpec(memory_space=pl.ANY)
    return pl.pallas_call(
        factor_kernel,
        out_shape=(
            jax.ShapeDtypeStruct((BLOCKS, B, B), F32),
            jax.ShapeDtypeStruct((B, B), F32),
        ),
        in_specs=[whole, any_space],
        out_specs=(any_space, whole),
        scratch_shapes=[
            pltpu.VMEM((B, B), F32),
            pltpu.VMEM((B, B), F32),
            pltpu.VMEM((BLOCKS, B, B), F32),
            pltpu.VMEM((BLOCKS, B, B), F32),
            pltpu.SemaphoreType.DMA((1 + BLOCKS,)),
        ],
        compiler_params=pltpu.CompilerParams(vmem_limit_bytes=58 * 1024 * 1024),
    )(gram, second)


def body(sketch, band_tiles, far_tiles, far_owner, far_local, far_count):
    second, gram = power_step(sketch, band_tiles, far_tiles, far_owner, far_local, far_count)
    return orthonormalize(gram, second)


def solution(mesh):
    in_specs = (
        P(("row", "grp"), None, None),
        P(("row", "grp"), None, None, None),
        P(("row", "grp"), None, None, None),
        P(("row", "grp"), None),
        P(("row", "grp"), None),
        P(("row", "grp")),
    )
    out_specs = (P(("row", "grp"), None, None), P())
    return jax.shard_map(body, mesh=mesh, in_specs=in_specs, out_specs=out_specs, check_vma=False)
```
